128 devices in a mesh: gx: 16 (over x, y), gy: 8 (over z, core).
Axes of the slice: x: 4, y: 4, z: 4, core: 2. Of those that a mesh axis runs over, the one named last changes fastest.
Arguments:
- dual_ops: float32 [16, 8, 1536, 1536], P('gx', 'gy')
- loads: float32 [16, 8, 2, 384, 128], P('gx', 'gy'), may hold values from -16 to 16
- coarse_rhs: float32 [16, 8, 6, 128], P('gx', 'gy'), may hold values from -288 to 288
- coarse_modes: float32 [16, 8, 2, 2, 6, 384], P('gx', 'gy'), as said below
- free_mask: int32 [16, 8, 2, 384], P('gx', 'gy'), may hold values from 0 to 1
- face_match: int32 [16, 8, 2, 384], P('gx', 'gy'), may hold values from 0 to 383, each once within a row
- coarse_rows: float32 [16, 8, 3, 6, 768], P('gx', 'gy'), as said below
Outputs:
- multipliers: float32 [16, 8, 2, 384, 128], P('gx', 'gy')
- projected: float32 [16, 8, 2, 384, 128], P('gx', 'gy')
The draws below stay inside these ranges and needn't reach their ends.
Inputs may be any that keep to these rules, and one draw needn't show every extreme that they name: The draws of coarse_modes, free_mask and coarse_rows belong together. coarse_modes[a,b,0,1] is zero on the last grid column and coarse_modes[a,b,1,1] on the last grid row. With C the symmetric positive definite coarse matrix whose entries are the sums of free times products of the coarse-mode images of two modes over all east and south face multipliers (G^T G restricted to free multipliers, in the order (a, b, mode)), coarse_rows[a,b,0] are the rows of the inverse of C for the modes of (a,b), up to rounding; coarse_rows[a,b,1] equals coarse_rows[a,b+1,0] and coarse_rows[a,b,2] equals coarse_rows[a+1,b,0], zero where that neighbour does not exist.
All inputs are finite; a program needn't handle non-finite values.
Results may differ from the reference program's by a relative error of at most 0.00029.
Values sent between devices are 32-bit elements; how exact they have to be, the bound alone decides.
No kernel may reach another device: no remote copies, remote signals or barrier semaphores. Data moves between devices by JAX's collectives and lax.ppermute only.
A program may use at most 64 MiB of HBM per device.

```python
import jax
import jax.numpy as jnp
from jax import lax

LM = 1536
LF = 384
ITERS = 3
NCASE = 128
SX = 16
SY = 8
NC = 768


def coarse_frame(key):
    base = jax.random.fold_in(key, 9173)
    key_dirs, key_plane, key_weight, key_mask, key_other = jax.random.split(base, 5)
    directions = jax.random.normal(key_dirs, (SX, SY, 2, LF, 3), jnp.float32)
    directions = directions / jnp.sqrt(jnp.sum(directions * directions, axis=-1, keepdims=True) + 1e-06)
    plane = jax.random.uniform(key_plane, (SX, SY, 2, LF, 2), jnp.float32, -0.5, 0.5)
    face_index = jnp.arange(2)[None, None, :, None]
    first = jnp.where(face_index == 0, 0.5, plane[..., 0])
    second = jnp.where(face_index == 0, plane[..., 0], 0.5)
    points = jnp.stack([first, second, plane[..., 1]], axis=-1)
    weights = jnp.exp(jax.random.uniform(key_weight, (SX, SY, 2, LF), jnp.float32, jnp.log(0.5), jnp.log(2.0)))
    other_weights = jnp.exp(jax.random.uniform(key_other, (SX, SY, 2, LF), jnp.float32, jnp.log(0.5), jnp.log(2.0)))

    def images_at(where, scale):
        rotation = jnp.cross(where, directions)
        return jnp.concatenate([directions, rotation], axis=-1) * scale[..., None]
    offsets = jnp.array([[1.0, 0.0, 0.0], [0.0, 1.0, 0.0]], jnp.float32)[None, None, :, None, :]
    own_images = images_at(points, weights)
    other_images = -images_at(points - offsets, other_weights)
    row_index = jnp.arange(SX)[:, None, None, None]
    col_index = jnp.arange(SY)[None, :, None, None]
    exists = jnp.where(face_index == 0, col_index < SY - 1, row_index < SX - 1)
    other_images = other_images * exists[..., None].astype(jnp.float32)
    modes = jnp.stack([own_images, other_images], axis=3)
    modes = jnp.transpose(modes, (0, 1, 2, 3, 5, 4))
    mask = (jax.random.randint(key_mask, (SX, SY, 2, LF), 0, 8) < 6).astype(jnp.int32)
    empty = jnp.zeros((SX, SY, 6, LF), jnp.float32)
    own_part = jnp.stack([modes[:, :, 0, 0], modes[:, :, 1, 0]], axis=3)
    east_part = jnp.stack([modes[:, :, 0, 1], empty], axis=3)
    south_part = jnp.stack([empty, modes[:, :, 1, 1]], axis=3)
    kernel = jnp.stack([own_part, east_part, south_part], axis=2)
    masked = kernel * mask[:, :, None, None, :, :].astype(jnp.float32)
    blocks = jnp.einsum('abrjfk,absifk->abrjsi', masked, kernel, precision=lax.Precision.HIGHEST)
    row_moves = [jnp.eye(SX, SX, 0), jnp.eye(SX, SX, 0), jnp.eye(SX, SX, 1)]
    col_moves = [jnp.eye(SY, SY, 0), jnp.eye(SY, SY, 1), jnp.eye(SY, SY, 0)]
    coarse = jnp.zeros((SX, SY, 6, SX, SY, 6), jnp.float32)
    for first_role in range(3):
        for second_role in range(3):
            coarse = coarse + jnp.einsum('abji,ac,bd,ae,bf->cdjefi', blocks[:, :, first_role, :, second_role, :], row_moves[first_role], col_moves[first_role], row_moves[second_role], col_moves[second_role], precision=lax.Precision.HIGHEST)
    coarse = coarse.reshape(NC, NC)
    inverse = jnp.linalg.inv(coarse)
    identity = jnp.eye(NC, dtype=jnp.float32)
    inverse = jnp.dot(inverse, 2.0 * identity - jnp.dot(coarse, inverse, precision=lax.Precision.HIGHEST), precision=lax.Precision.HIGHEST)
    inverse = 0.5 * (inverse + inverse.T)
    grid_rows = inverse.reshape(SX, SY, 6, NC)
    padded = jnp.pad(grid_rows, ((0, 1), (0, 1), (0, 0), (0, 0)))
    rows = jnp.stack([grid_rows, padded[:SX, 1:SY + 1], padded[1:SX + 1, :SY]], axis=2)
    return (modes, mask, rows)


def draw_coarse_modes(key, part):
    return coarse_frame(key)[0]


def draw_free_mask(key, part):
    return coarse_frame(key)[1]


def draw_coarse_rows(key, part):
    return coarse_frame(key)[2]


def draw_dual_ops(key, part):
    base = jax.random.fold_in(key, 31)
    key_noise, key_diag, key_scale = jax.random.split(base, 3)
    noise = jax.random.normal(key_noise, (SX, SY, LM, LM), jnp.float32)
    noise = (noise + jnp.swapaxes(noise, 2, 3)) / jnp.sqrt(2.0 * LM)
    diagonal = jax.random.uniform(key_diag, (SX, SY, LM), jnp.float32, 2.5, 4.0)
    scales = jnp.exp(jax.random.uniform(key_scale, (SX, SY, LM), jnp.float32, jnp.log(0.5), jnp.log(2.0)))
    matrix = noise + diagonal[..., None] * jnp.eye(LM, dtype=jnp.float32)
    return scales[..., :, None] * scales[..., None, :] * matrix


def draw_loads(key, part):
    base = jax.random.fold_in(key, 57)
    position = (jnp.arange(SX)[:, None] * SY + jnp.arange(SY)[None, :]).astype(jnp.float32) / (SX * SY - 1)
    values = jax.random.truncated_normal(base, -4.0, 4.0, (SX, SY, 2, LF, NCASE), jnp.float32)
    ramp = jnp.power(3.0, position)
    return values * ramp[:, :, None, None, None]


def level_of(stream_key, dims, pieces, least, largest):
    def one(dim, parts):
        steps = jax.random.uniform(jax.random.fold_in(jax.random.fold_in(stream_key, 6), dim), (parts,), jnp.float32, least / len(pieces), largest / len(pieces))
        return jnp.repeat(jnp.exp(steps), dims[dim] // parts).reshape((-1,) + (1,) * (len(dims) - dim - 1))

    factor_of = one(*pieces[0])
    for cut in pieces[1:]:
        factor_of = factor_of * one(*cut)
    return factor_of


def scatter_about(own_key, dims, deviation, bound, cuts=(), kind=jnp.bfloat16):
    drawn = jax.random.normal(own_key, dims, jnp.float32) * deviation
    if len(cuts) > 0:
        drawn = level_of(own_key, dims, cuts, -0.22, 0.18) * drawn
    return jnp.clip(drawn, min=-bound, max=bound).astype(kind)


def setup_inputs(seed: int = 0) -> dict:
    arg_keys = jax.random.split(jax.random.key(seed), 8)
    dual_ops = draw_dual_ops(jax.random.fold_in(arg_keys[7], 71), 0)
    loads = draw_loads(jax.random.fold_in(arg_keys[7], 71), 0)
    coarse_rhs = scatter_about(arg_keys[2], (SX, SY, 6, NCASE), (LF // 8), 288.0, ((0, 16), (1, 8)), jnp.float32)
    coarse_modes = draw_coarse_modes(jax.random.fold_in(arg_keys[7], 71), 0)
    free_mask = draw_free_mask(jax.random.fold_in(arg_keys[7], 71), 0)
    face_match = jax.vmap(lambda own: jax.random.permutation(own, LF))(jax.random.split(arg_keys[5], SX * SY * 2)).reshape((SX, SY, 2, LF)).astype(jnp.int32)
    coarse_rows = draw_coarse_rows(jax.random.fold_in(arg_keys[7], 71), 0)
    return dict(dual_ops=dual_ops, loads=loads, coarse_rhs=coarse_rhs, coarse_modes=coarse_modes, free_mask=free_mask, face_match=face_match, coarse_rows=coarse_rows)


HIGHEST = lax.Precision.HIGHEST

def lower_shift(values, dimension):
    widths = [(0, 0)] * values.ndim
    widths[dimension] = (1, 0)
    return lax.slice_in_dim(jnp.pad(values, widths), 0, values.shape[dimension], axis=dimension)

def upper_shift(values, dimension):
    widths = [(0, 0)] * values.ndim
    widths[dimension] = (0, 1)
    return lax.slice_in_dim(jnp.pad(values, widths), 1, values.shape[dimension] + 1, axis=dimension)

def pick_rows(values, indices):
    full_index = jnp.broadcast_to(indices[..., None], values.shape)
    return jnp.take_along_axis(values, full_index, axis=2)

def apply_dual(dual_ops, face_match, free_slots, field):
    face_slots = field.shape[3]
    case_count = field.shape[4]
    from_west = lower_shift(field[:, :, 0], 1)
    from_north = lower_shift(field[:, :, 1], 0)
    west_side = -pick_rows(from_west, face_match[:, :, 0])
    north_side = -pick_rows(from_north, face_match[:, :, 1])
    stacked = jnp.concatenate([field[:, :, 0], field[:, :, 1], west_side, north_side], axis=2)
    product = jnp.einsum('abij,abjc->abic', dual_ops, stacked, precision=HIGHEST)
    product = product.reshape(product.shape[0], product.shape[1], 4, face_slots, case_count)
    inverse = jnp.argsort(face_match, axis=-1).astype(jnp.int32)
    back_west = upper_shift(pick_rows(product[:, :, 2], inverse[:, :, 0]), 1)
    back_north = upper_shift(pick_rows(product[:, :, 3], inverse[:, :, 1]), 0)
    return (product[:, :, :2] - jnp.stack([back_west, back_north], axis=2)) * free_slots

def coarse_terms(coarse_modes, field):
    own_terms = jnp.einsum('abfjk,abfkc->abjc', coarse_modes[:, :, :, 0], field, precision=HIGHEST)
    east_terms = jnp.einsum('abjk,abkc->abjc', coarse_modes[:, :, 0, 1], field[:, :, 0], precision=HIGHEST)
    south_terms = jnp.einsum('abjk,abkc->abjc', coarse_modes[:, :, 1, 1], field[:, :, 1], precision=HIGHEST)
    return (own_terms, east_terms, south_terms)

def coarse_solve(coarse_rows, own_terms, east_terms, south_terms):
    summed = own_terms + lower_shift(east_terms, 1) + lower_shift(south_terms, 0)
    flat = summed.reshape(-1, summed.shape[-1])
    return jnp.einsum('abrjn,nc->abrjc', coarse_rows, flat, precision=HIGHEST)

def mode_images(coarse_modes, free_slots, alpha):
    east_face = jnp.einsum('abjk,abjc->abkc', coarse_modes[:, :, 0, 0], alpha[:, :, 0], precision=HIGHEST)
    east_face = east_face + jnp.einsum('abjk,abjc->abkc', coarse_modes[:, :, 0, 1], alpha[:, :, 1], precision=HIGHEST)
    south_face = jnp.einsum('abjk,abjc->abkc', coarse_modes[:, :, 1, 0], alpha[:, :, 0], precision=HIGHEST)
    south_face = south_face + jnp.einsum('abjk,abjc->abkc', coarse_modes[:, :, 1, 1], alpha[:, :, 2], precision=HIGHEST)
    return jnp.stack([east_face, south_face], axis=2) * free_slots

def reference(dual_ops, loads, coarse_rhs, coarse_modes, free_mask, face_match, coarse_rows):
    free_slots = free_mask.astype(jnp.float32)[..., None]

    def project(field):
        own_terms, east_terms, south_terms = coarse_terms(coarse_modes, field)
        alpha = coarse_solve(coarse_rows, own_terms, east_terms, south_terms)
        return field - mode_images(coarse_modes, free_slots, alpha)
    zeros_rhs = jnp.zeros_like(coarse_rhs)
    multipliers = mode_images(coarse_modes, free_slots, coarse_solve(coarse_rows, coarse_rhs, zeros_rhs, zeros_rhs))
    gradient = apply_dual(dual_ops, face_match, free_slots, multipliers) - loads * free_slots
    projected = project(gradient)
    norm_now = jnp.sum(projected * projected, axis=(0, 1, 2, 3))
    direction = projected
    for step in range(ITERS):
        image = apply_dual(dual_ops, face_match, free_slots, direction)
        step_size = norm_now / jnp.sum(direction * image, axis=(0, 1, 2, 3))
        multipliers = multipliers + step_size * direction
        gradient = gradient + step_size * image
        projected = project(gradient)
        norm_next = jnp.sum(projected * projected, axis=(0, 1, 2, 3))
        if step + 1 < ITERS:
            direction = projected + norm_next / norm_now * direction
            norm_now = norm_next
    return (multipliers, projected)
```

```python
import functools

import jax
import jax.numpy as jnp
import numpy as np
from jax import lax
from jax.experimental import pallas as pl
from jax.experimental.pallas import tpu as pltpu
from jax.sharding import PartitionSpec as P

F32 = jnp.float32
BF16 = jnp.bfloat16
HIGHEST = lax.Precision.HIGHEST
MODES = 6
GROUP = 8
MEMBERS = 5
ROWS = GROUP * MEMBERS
TROWS = 48
NORM_ROW, ENERGY_ROW, CROSS_ROW = 6, 7, 14


def params(megabytes):
    return pltpu.CompilerParams(vmem_limit_bytes=megabytes * 1024 * 1024)


def split(value):
    high = value.astype(BF16)
    low = (value - high.astype(F32)).astype(BF16)
    return high, low


def mm(left, right):
    return jnp.dot(left, right, preferred_element_type=F32)


def both(value):
    high, low = split(value)
    return jnp.concatenate([high, low], axis=1)


def mm3(left_high, left_low, pair):
    columns = pair.shape[1] // 2
    wide = mm(left_high, pair)
    return wide[:, :columns] + wide[:, columns:] + mm(left_low, pair[:, :columns])


def fold_kernel(match_ref, operator_ref, high_ref, low_ref):
    face = pl.program_id(0)
    slots = match_ref.shape[1]
    order = lax.broadcasted_iota(jnp.int32, (slots, slots), 0)

    def moves(side):
        return jnp.where(order == match_ref[side : side + 1, :], 1.0, 0.0).astype(BF16)

    def columns(parts, near, far):
        for part, out in zip(parts, (high_ref, low_ref)):
            own = part[:, : 2 * slots]
            out[:, : 2 * slots] = own if near > 0 else -own
            for side in range(2):
                piece = part[:, (2 + side) * slots : (3 + side) * slots]
                moved = lax.dot_general(
                    piece, moves(side), (((1,), (1,)), ((), ())), preferred_element_type=F32
                )
                out[:, (2 + side) * slots : (3 + side) * slots] = (far * moved).astype(BF16)

    @pl.when(face < 2)
    def _():
        columns(split(operator_ref[...]), 1.0, -1.0)

    for side in range(2):

        @pl.when(face == 2 + side)
        def _(side=side):
            pick = moves(side)
            parts = split(operator_ref[...])
            columns([mm(pick, part).astype(BF16) for part in parts], -1.0, 1.0)


def fold(operator, match):
    size = operator.shape[0]
    slots = match.shape[1]
    block = pl.BlockSpec((slots, size), lambda i: (i, 0))
    return pl.pallas_call(
        fold_kernel,
        grid=(size // slots,),
        in_specs=[pl.BlockSpec((2, slots), lambda i: (0, 0)), block],
        out_specs=[block, block],
        out_shape=[jax.ShapeDtypeStruct((size, size), BF16)] * 2,
        compiler_params=params(48),
        name="fold",
    )(match, operator)


def pack_kernel(rows_ref, modes_ref, free_ref, rhs_ref, east_ref, south_ref, message_ref):
    slots = free_ref.shape[1]
    for face, out in enumerate((east_ref, south_ref)):
        out[...] = jnp.zeros_like(out)
        out[0:MODES, :] = rows_ref[0]
        out[6:7, :slots] = free_ref[face : face + 1, :].astype(F32)
        for side in range(2):
            out[8 : 8 + MODES, side * slots : (side + 1) * slots] = modes_ref[face, side]
    message_ref[...] = jnp.zeros_like(message_ref)
    for peer in range(message_ref.shape[0]):
        message_ref[peer, 0:MODES, :] = rhs_ref[...]


def pack(rows, modes, free, rhs, peers):
    width = rows.shape[-1]
    return pl.pallas_call(
        pack_kernel,
        out_shape=[
            jax.ShapeDtypeStruct((16, width), F32),
            jax.ShapeDtypeStruct((16, width), F32),
            jax.ShapeDtypeStruct((peers, GROUP, rhs.shape[-1]), F32),
        ],
        name="pack",
    )(rows, modes, free, rhs)


def frame_kernel(
    lines, modes_ref, free_ref, rows_ref, west_ref, north_ref,
    mask_ref, t_high_ref, t_low_ref, g_high_ref, g_low_ref, coarse_ref, pieces_ref, table_ref,
):
    slots = free_ref.shape[1]
    cases = mask_ref.shape[1]
    span = MODES * lines[1]
    table_ref[...] = jnp.zeros_like(table_ref)
    masks = [
        free_ref[0:1, :].astype(F32), free_ref[1:2, :].astype(F32),
        west_ref[6:7, :slots], north_ref[6:7, :slots],
    ]
    entries = [
        (0, 0, modes_ref[0, 0]), (0, 1, modes_ref[1, 0]),
        (1, 0, modes_ref[0, 1]), (2, 1, modes_ref[1, 1]),
        (3, 2, west_ref[8 : 8 + MODES, :slots]), (0, 2, west_ref[8 : 8 + MODES, slots : 2 * slots]),
        (4, 3, north_ref[8 : 8 + MODES, :slots]), (0, 3, north_ref[8 : 8 + MODES, slots : 2 * slots]),
    ]
    for member, face, values in entries:
        table_ref[member * GROUP : member * GROUP + MODES, face * slots : (face + 1) * slots] = (
            values * masks[face]
        )
    table = table_ref[...]
    high, low = split(table[:TROWS])
    t_high_ref[...] = high
    t_low_ref[...] = low
    high, low = split(table.T)
    g_high_ref[...] = high
    g_low_ref[...] = low
    for face in range(4):
        spread = jnp.broadcast_to(masks[face], (cases, slots))
        mask_ref[face * slots : (face + 1) * slots, :] = spread.T
    coarse_ref[...] = jnp.zeros_like(coarse_ref)
    members = [rows_ref[0], rows_ref[1], rows_ref[2], west_ref[0:MODES, :], north_ref[0:MODES, :]]
    for member, values in enumerate(members):
        coarse_ref[member * GROUP : member * GROUP + MODES, :] = values
    edge = jnp.zeros((ROWS, span), F32)
    padded = jnp.concatenate([edge, coarse_ref[...], edge], axis=1)
    rest = jnp.zeros((ROWS, pieces_ref.shape[2] - 3 * span), F32)
    for line in range(lines[0]):
        piece = padded[:, line * span : (line + 3) * span]
        pieces_ref[line] = jnp.concatenate([piece, rest], axis=1)


def frame(lines, modes, free, rows, west, north, cases):
    slots = free.shape[1]
    size = 4 * slots
    width = rows.shape[-1]
    return pl.pallas_call(
        functools.partial(frame_kernel, lines),
        out_shape=[
            jax.ShapeDtypeStruct((size, cases), F32),
            jax.ShapeDtypeStruct((TROWS, size), BF16),
            jax.ShapeDtypeStruct((TROWS, size), BF16),
            jax.ShapeDtypeStruct((size, 128), BF16),
            jax.ShapeDtypeStruct((size, 128), BF16),
            jax.ShapeDtypeStruct((ROWS, width), F32),
            jax.ShapeDtypeStruct((lines[0], ROWS, 256), F32),
        ],
        scratch_shapes=[pltpu.VMEM((128, size), F32)],
        compiler_params=params(32),
        name="frame",
    )(modes, free, rows, west, north)


def expansion(lines):
    span = MODES * lines[1]
    out = np.zeros((256, lines[1] * ROWS), np.float32)
    for source in range(lines[1]):
        places = [(0, source), (0, source + 1), (1, source), (0, source - 1), (-1, source)]
        for member, (down, column) in enumerate(places):
            if 0 <= column < lines[1]:
                for mode in range(MODES):
                    at = span * (1 + down) + MODES * column + mode
                    out[at, source * ROWS + member * GROUP + mode] = 1.0
    return jnp.asarray(out, BF16)


def spread_kernel(received_ref, expand_ref, high_ref, low_ref):
    flat = received_ref[...].reshape(high_ref.shape[0], received_ref.shape[2])
    for part, out in zip(split(flat), (high_ref, low_ref)):
        out[...] = mm(part, expand_ref[...]).astype(BF16)


def spread(received, expand):
    shape = (received.shape[0] * ROWS, expand.shape[1])
    return pl.pallas_call(
        spread_kernel,
        out_shape=[jax.ShapeDtypeStruct(shape, BF16)] * 2,
        name="spread",
    )(received, expand)


def solve_kernel(terms_ref, high_ref, low_ref, out_ref):
    terms = terms_ref[...]
    peers, rows, cases = terms.shape
    result = mm3(high_ref[...], low_ref[...], both(terms.reshape(peers * rows, cases)))
    result = result.reshape(out_ref.shape)
    total = jnp.sum(terms, axis=0)
    place = lax.broadcasted_iota(jnp.int32, (rows, cases), 0)
    scalar = (place % GROUP) >= MODES
    out_ref[...] = jnp.where(scalar[None], total[None], result)


def solve(terms, high, low):
    lines = high.shape[0] // ROWS
    return pl.pallas_call(
        solve_kernel,
        out_shape=jax.ShapeDtypeStruct((lines, ROWS, terms.shape[2]), F32),
        name="solve",
    )(terms, high, low)


def lift(alpha, g_high_ref, g_low_ref):
    filler = jnp.zeros((g_high_ref.shape[1] - alpha.shape[0], alpha.shape[1]), F32)
    pair = both(jnp.concatenate([alpha, filler], axis=0))
    return mm3(g_high_ref[...], g_low_ref[...], pair)


def field_image(z_ref, halo_refs, mask_ref, even_x, even_y, faces=4):
    x_first, x_second, y_first, y_second = halo_refs
    received = [
        jnp.where(even_y, y_first[...], y_second[...]),
        jnp.where(even_x, x_first[...], x_second[...]),
    ]
    if faces == 4:
        received.append(jnp.where(even_y, y_second[...], y_first[...]))
        received.append(jnp.where(even_x, x_second[...], x_first[...]))
    slots = received[0].shape[0]
    return jnp.concatenate(
        [
            mask_ref[f * slots : (f + 1) * slots, :] * (z_ref[f] + received[f])
            for f in range(faces)
        ],
        axis=0,
    )


def member_alpha(total):
    place = lax.broadcasted_iota(jnp.int32, total.shape, 0)
    return jnp.where((place % GROUP) < MODES, total, 0.0)


def step_kernel(phase, names, *refs):
    r = dict(zip(names, refs))
    face = pl.program_id(0)
    even_x = r["parity"][0] == 0
    even_y = r["parity"][1] == 0
    slots = r["a_high"].shape[0]
    half = 2 * slots

    @pl.when(face == 0)
    def _():
        r["terms"][...] = jnp.zeros_like(r["terms"])
        if phase == 0:
            alpha = jnp.dot(
                r["coarse"][...], r["rhs"][...], precision=HIGHEST, preferred_element_type=F32
            )
            field = lift(alpha, r["g_high"], r["g_low"])
            r["lam_out"][...] = field[:half]
        else:
            total = jnp.sum(r["parts"][...], axis=0)
            halos = (r["x_first"], r["x_second"], r["y_first"], r["y_second"])
            image = field_image(r["z"], halos, r["mask"], even_x, even_y)
            moved = image - lift(member_alpha(total), r["g_high"], r["g_low"])
            if phase == 1:
                field = moved
            elif phase == 2:
                norm = total[NORM_ROW : NORM_ROW + 1, :]
                energy = total[ENERGY_ROW : ENERGY_ROW + 1, :]
                step = norm / energy
                field = r["p"][...] + step * moved
                r["q_out"][...] = moved
                r["lam_out"][...] = r["lam"][...] + step * r["p"][:half, :]
                r["scal_out"][0:1, :] = norm
                r["scal_out"][1:2, :] = energy
            else:
                step, beta, curvature, norm = step_terms(total, r["scal"])
                direction = r["p"][...] + beta * r["d"][...]
                image_p = moved + beta * r["q"][...]
                field = r["p"][...] + step * image_p
                r["d_out"][...] = direction
                r["q_out"][...] = image_p
                r["lam_out"][...] = r["lam"][...] + step * direction[:half]
                r["scal_out"][0:1, :] = norm
                r["scal_out"][1:2, :] = curvature
                for f in range(4):
                    r["zd_out"][f] = r["z"][f] + beta * r["zd"][f]
        if phase >= 1:
            r["p_out"][...] = field
            r["norm"][...] = jnp.sum(field[:half] * field[:half], axis=0, keepdims=True)
            r["energy"][...] = jnp.zeros_like(r["energy"])
            r["cross"][...] = jnp.zeros_like(r["cross"])
        r["pair"][...] = both(field)

    out = mm3(r["a_high"][...], r["a_low"][...], r["pair"][...])
    if phase == 0:
        out = out - jnp.where(face < 2, r["loads"][jnp.minimum(face, 1)], 0.0)
    r["z_out"][0] = out
    r["terms"][...] += mm3(r["t_high"][...], r["t_low"][...], both(out))
    if phase >= 1:
        rows = pl.ds(pl.multiple_of(face * slots, slots), slots)
        mine = r["p_out"][rows, :]
        r["energy"][...] += jnp.sum(mine * out, axis=0, keepdims=True)
        if phase == 2:
            cross = mine * r["z"][face] + r["p"][rows, :] * out
            r["cross"][...] += jnp.sum(cross, axis=0, keepdims=True)
        elif phase == 3:
            cross = mine * r["zd_out"][face] + r["d_out"][rows, :] * out
            r["cross"][...] += jnp.sum(cross, axis=0, keepdims=True)

    for target, even, first, second in (
        ("send_x_first", even_x, 1, 3), ("send_x_second", even_x, 3, 1),
        ("send_y_first", even_y, 0, 2), ("send_y_second", even_y, 2, 0),
    ):

        @pl.when(face == jnp.where(even, first, second))
        def _(target=target):
            r[target][...] = out

    @pl.when(face == 3)
    def _():
        terms = r["terms"][0:ROWS, :]
        if phase >= 1:
            place = lax.broadcasted_iota(jnp.int32, terms.shape, 0)
            terms = jnp.where(place == NORM_ROW, r["norm"][...], terms)
            terms = jnp.where(place == ENERGY_ROW, r["energy"][...], terms)
            terms = jnp.where(place == CROSS_ROW, r["cross"][...], terms)
        for peer in range(r["message"].shape[0]):
            r["message"][peer] = terms


def step_terms(total, scal_ref):
    norm = total[NORM_ROW : NORM_ROW + 1, :]
    energy = total[ENERGY_ROW : ENERGY_ROW + 1, :]
    cross = total[CROSS_ROW : CROSS_ROW + 1, :]
    beta = norm / scal_ref[0:1, :]
    curvature = energy + beta * cross + beta * beta * scal_ref[1:2, :]
    return norm / curvature, beta, curvature, norm


def step(phase, peers, operator, table, inputs):
    a_high, a_low = operator
    size = a_high.shape[0]
    slots = size // 4
    cases = 128
    values = dict(inputs)
    values.update(a_high=a_high, a_low=a_low, t_high=table[0], t_low=table[1])
    specs = []
    for name, value in values.items():
        if name == "parity":
            specs.append(pl.BlockSpec(memory_space=pltpu.SMEM))
        elif name in ("a_high", "a_low"):
            specs.append(pl.BlockSpec((slots, size), lambda i: (i, 0)))
        elif name in ("t_high", "t_low"):
            specs.append(pl.BlockSpec((TROWS, slots), lambda i: (0, i)))
        else:
            specs.append(whole(value.shape))
    shapes = {
        "z_out": (4, slots, cases),
        "send_x_first": (slots, cases), "send_x_second": (slots, cases),
        "send_y_first": (slots, cases), "send_y_second": (slots, cases),
        "message": (peers, ROWS, cases),
    }
    if phase in (0, 2, 3):
        shapes["lam_out"] = (2 * slots, cases)
    if phase >= 1:
        shapes["p_out"] = (size, cases)
    if phase >= 2:
        shapes["q_out"] = (size, cases)
    if phase == 3:
        shapes["d_out"] = (size, cases)
        shapes["zd_out"] = (4, slots, cases)
    if phase >= 2:
        shapes["scal_out"] = (8, cases)
    out_specs = []
    for name, shape in shapes.items():
        if name == "z_out":
            out_specs.append(pl.BlockSpec((1, slots, cases), lambda i: (i, 0, 0)))
        else:
            out_specs.append(whole(shape))
    scratch = {
        "pair": pltpu.VMEM((size, 2 * cases), BF16),
        "terms": pltpu.VMEM((TROWS, cases), F32),
        "norm": pltpu.VMEM((1, cases), F32),
        "energy": pltpu.VMEM((1, cases), F32),
        "cross": pltpu.VMEM((1, cases), F32),
    }
    names = list(values) + list(shapes) + list(scratch)
    outs = pl.pallas_call(
        functools.partial(step_kernel, phase, names),
        grid=(4,),
        in_specs=specs,
        out_specs=out_specs,
        out_shape=[jax.ShapeDtypeStruct(shape, F32) for shape in shapes.values()],
        scratch_shapes=list(scratch.values()),
        compiler_params=params(48),
        name=f"step{phase}",
    )(*values.values())
    return dict(zip(shapes, outs))


def whole(shape):
    return pl.BlockSpec(shape, lambda i, rank=len(shape): (0,) * rank)


def final_kernel(names, *refs):
    r = dict(zip(names, refs))
    even_x = r["parity"][0] == 0
    even_y = r["parity"][1] == 0
    half = r["lam"].shape[0]
    total = jnp.sum(r["parts"][...], axis=0)
    halos = (r["x_first"], r["x_second"], r["y_first"], r["y_second"])
    image = field_image(r["z"], halos, r["mask"], even_x, even_y, faces=2)
    moved = image - lift(member_alpha(total), r["g_high"], r["g_low"])
    step_size, beta, _, _ = step_terms(total, r["scal"])
    direction = r["p"][...] + beta * r["d"][...]
    r["lam_out"][...] = r["lam"][...] + step_size * direction
    r["p_out"][...] = r["p"][...] + step_size * (moved + beta * r["q"][...])


def final(inputs):
    half, cases = inputs["lam"].shape
    slots = half // 2
    specs = []
    for name, value in inputs.items():
        if name == "parity":
            specs.append(pl.BlockSpec(memory_space=pltpu.SMEM))
        elif name in ("z",):
            specs.append(pl.BlockSpec((2, slots, cases), lambda i: (0, 0, 0)))
        elif name in ("mask", "g_high", "g_low", "p", "d", "q"):
            specs.append(pl.BlockSpec((half, value.shape[1]), lambda i: (0, 0)))
        else:
            specs.append(whole(value.shape))
    names = list(inputs) + ["lam_out", "p_out"]
    return pl.pallas_call(
        functools.partial(final_kernel, names),
        grid=(1,),
        in_specs=specs,
        out_specs=[whole((half, cases))] * 2,
        out_shape=[jax.ShapeDtypeStruct((half, cases), F32)] * 2,
        compiler_params=params(32),
        name="final",
    )(*inputs.values())


def swap_first(peers):
    return [(i, i ^ 1) for i in range(peers)]


def swap_second(peers):
    return [(i, i + 1 if i % 2 else i - 1) for i in range(1, peers - 1)]


def local(dual_ops, loads, coarse_rhs, coarse_modes, free_mask, face_match, coarse_rows):
    operator = dual_ops[0, 0]
    modes = coarse_modes[0, 0]
    free = free_mask[0, 0]
    rows = coarse_rows[0, 0]
    slots, cases = loads.shape[-2:]
    lines = (lax.axis_size("gx"), lax.axis_size("gy"))
    peers = lines[0] * lines[1]
    parity = jnp.stack([lax.axis_index("gx") % 2, lax.axis_index("gy") % 2]).astype(jnp.int32)

    pack_east, pack_south, message = pack(rows, modes, free, coarse_rhs[0, 0], peers)
    west = lax.ppermute(pack_east, "gy", [(i, i + 1) for i in range(lines[1] - 1)])
    north = lax.ppermute(pack_south, "gx", [(i, i + 1) for i in range(lines[0] - 1)])
    gathered = lax.all_to_all(message, ("gx", "gy"), 0, 0)
    rhs = gathered[:, :MODES].reshape(peers * MODES, cases)
    folded = fold(operator, face_match[0, 0])
    mask, t_high, t_low, g_high, g_low, coarse, pieces = frame(
        lines, modes, free, rows, west, north, cases
    )
    received = lax.all_to_all(pieces, "gx", 0, 0)
    solver = spread(received, expansion(lines))

    def exchange(out):
        halo = {
            "x_first": lax.ppermute(out["send_x_first"], "gx", swap_first(lines[0])),
            "x_second": lax.ppermute(out["send_x_second"], "gx", swap_second(lines[0])),
            "y_first": lax.ppermute(out["send_y_first"], "gy", swap_first(lines[1])),
            "y_second": lax.ppermute(out["send_y_second"], "gy", swap_second(lines[1])),
        }
        terms = lax.all_to_all(out["message"], "gy", 0, 0)
        parts = lax.all_to_all(solve(terms, *solver), "gx", 0, 0)
        return dict(parity=parity, parts=parts, z=out["z_out"], mask=mask, g_high=g_high, g_low=g_low, **halo)

    table = (t_high, t_low)
    start = step(
        0, lines[1], folded, table,
        dict(parity=parity, rhs=rhs, coarse=coarse, g_high=g_high, g_low=g_low, loads=loads[0, 0]),
    )
    first = step(1, lines[1], folded, table, exchange(start))
    second = step(
        2, lines[1], folded, table, dict(exchange(first), p=first["p_out"], lam=start["lam_out"])
    )
    third = step(
        3, lines[1], folded, table,
        dict(
            exchange(second), p=second["p_out"], d=first["p_out"], q=second["q_out"],
            zd=first["z_out"], scal=second["scal_out"], lam=second["lam_out"],
        ),
    )
    multipliers, projected = final(
        dict(
            exchange(third), p=third["p_out"], d=third["d_out"], q=third["q_out"],
            scal=third["scal_out"], lam=third["lam_out"],
        )
    )
    shape = (1, 1, 2, slots, cases)
    return multipliers.reshape(shape), projected.reshape(shape)


def solution(mesh):
    in_specs = (
        P("gx", "gy", None, None),
        P("gx", "gy", None, None, None),
        P("gx", "gy", None, None),
        P("gx", "gy", None, None, None, None),
        P("gx", "gy", None, None),
        P("gx", "gy", None, None),
        P("gx", "gy", None, None, None),
    )
    out_specs = (P("gx", "gy", None, None, None), P("gx", "gy", None, None, None))
    return jax.shard_map(local, mesh=mesh, in_specs=in_specs, out_specs=out_specs, check_vma=False)
```

```python
import functools
from types import SimpleNamespace

import jax
import jax.numpy as jnp
import numpy as np
from jax import lax
from jax.experimental import pallas as pl
from jax.experimental.pallas import tpu as pltpu
from jax.sharding import PartitionSpec as P

F32 = jnp.float32
BF16 = jnp.bfloat16
HIGHEST = lax.Precision.HIGHEST
MODES = 6
GROUP = 8
MEMBERS = 5
ROWS = GROUP * MEMBERS
TROWS = 48
LAST = 3
FLAGS = 6
KEPT = 3 * GROUP
TAIL = 16
STEP_MB = 16
NORM_ROW, ENERGY_ROW, CROSS_ROW = 6, 7, 14


VMEM_SPEC = pl.BlockSpec(memory_space=pltpu.VMEM)
SMEM_SPEC = pl.BlockSpec(memory_space=pltpu.SMEM)


def params(megabytes):
    return pltpu.CompilerParams(vmem_limit_bytes=megabytes * 1024 * 1024)


def split(value):
    high = value.astype(BF16)
    low = (value - high.astype(F32)).astype(BF16)
    return high, low


def mm(left, right):
    return jnp.dot(left, right, preferred_element_type=F32)


def both(value):
    high, low = split(value)
    return jnp.concatenate([high, low], axis=1)


def mm3(left_high, left_low, pair):
    columns = pair.shape[1] // 2
    wide = mm(left_high, pair)
    return wide[:, :columns] + wide[:, columns:] + mm(left_low, pair[:, :columns])


def pack_kernel(rows_ref, modes_ref, free_ref, rhs_ref, east_ref, south_ref, message_ref):
    slots = free_ref.shape[1]
    for face, out in enumerate((east_ref, south_ref)):
        out[...] = jnp.zeros_like(out)
        out[0:MODES, :] = rows_ref[0]
        out[6:7, :slots] = free_ref[face : face + 1, :].astype(F32)
        for side in range(2):
            out[8 : 8 + MODES, side * slots : (side + 1) * slots] = modes_ref[face, side]
    message_ref[...] = jnp.zeros_like(message_ref)
    for peer in range(message_ref.shape[0]):
        message_ref[peer, 0:MODES, :] = rhs_ref[...]


def pack(rows, modes, free, rhs, peers):
    width = rows.shape[-1]
    return pl.pallas_call(
        pack_kernel,
        in_specs=[VMEM_SPEC] * 4,
        out_specs=[VMEM_SPEC] * 3,
        out_shape=[
            jax.ShapeDtypeStruct((16, width), F32),
            jax.ShapeDtypeStruct((16, width), F32),
            jax.ShapeDtypeStruct((peers, GROUP, rhs.shape[-1]), F32),
        ],
        compiler_params=params(8),
        name="pack",
    )(rows, modes, free, rhs)


def frame_kernel(
    lines, place_ref, modes_ref, free_ref, match_ref, rows_ref, west_ref, north_ref, rhs_ref,
    mask_ref, t_high_ref, t_low_ref, g_high_ref, g_low_ref, gives_ref, takes_ref,
    coarse_ref, pieces_ref, table_ref, held_ref,
):
    slots = free_ref.shape[1]
    cases = mask_ref.shape[1]
    span = MODES * lines[1]
    no_north, no_west = place_ref[4] != 0, place_ref[5] != 0
    west = jnp.where(no_west, 0.0, west_ref[...])
    north = jnp.where(no_north, 0.0, north_ref[...])
    table_ref[...] = jnp.zeros_like(table_ref)
    masks = [
        free_ref[0:1, :].astype(F32), free_ref[1:2, :].astype(F32),
        west[6:7, :slots], north[6:7, :slots],
    ]
    entries = [
        (0, 0, modes_ref[0, 0]), (0, 1, modes_ref[1, 0]),
        (1, 0, modes_ref[0, 1]), (2, 1, modes_ref[1, 1]),
        (3, 2, west[8 : 8 + MODES, :slots]), (0, 2, west[8 : 8 + MODES, slots : 2 * slots]),
        (4, 3, north[8 : 8 + MODES, :slots]), (0, 3, north[8 : 8 + MODES, slots : 2 * slots]),
    ]
    for member, face, values in entries:
        table_ref[member * GROUP : member * GROUP + MODES, face * slots : (face + 1) * slots] = (
            values * masks[face]
        )
    table = table_ref[...]
    high, low = split(table[:TROWS])
    t_high_ref[...] = high
    t_low_ref[...] = low
    high, low = split(table.T)
    g_high_ref[...] = high
    g_low_ref[...] = low
    for face in range(4):
        spread = jnp.broadcast_to(masks[face], (cases, slots))
        mask_ref[face * slots : (face + 1) * slots, :] = spread.T
    order = lax.broadcasted_iota(jnp.int32, (slots, slots), 0)
    for side in range(2):
        moves = jnp.where(order == match_ref[side : side + 1, :], 1.0, 0.0)
        gives_ref[side] = moves.astype(BF16)
        takes_ref[side] = moves.T.astype(BF16)
    coarse_ref[...] = jnp.zeros_like(coarse_ref)
    members = [rows_ref[0], rows_ref[1], rows_ref[2], west[0:MODES, :], north[0:MODES, :]]
    for member, values in enumerate(members):
        coarse_ref[member * GROUP : member * GROUP + MODES, :] = values
    edge = jnp.zeros((ROWS, span), F32)
    padded = jnp.concatenate([edge, coarse_ref[...], edge], axis=1)
    for source in range(lines[1]):
        held_ref[source * MODES : (source + 1) * MODES, :] = rhs_ref[source, 0:MODES]
    tail = 3 * span - cases
    for line in range(lines[0]):
        first = line * span
        pieces_ref[line, 0:ROWS] = padded[:, first : first + cases]
        last = padded[:, first + cases : first + 3 * span]
        pieces_ref[line, ROWS : ROWS + GROUP] = jnp.zeros((GROUP, cases), F32)
        for member in range(MEMBERS):
            pieces_ref[line, ROWS : ROWS + GROUP, member * tail : (member + 1) * tail] = last[
                member * GROUP : (member + 1) * GROUP
            ]
        pieces_ref[line, ROWS + GROUP :] = held_ref[...]


def frame(lines, place, modes, free, match, rows, west, north, rhs):
    slots = free.shape[1]
    size = 4 * slots
    width = rows.shape[-1]
    cases = rhs.shape[-1]
    span = MODES * lines[1]
    return pl.pallas_call(
        functools.partial(frame_kernel, lines),
        in_specs=[SMEM_SPEC] + [VMEM_SPEC] * 7,
        out_specs=[VMEM_SPEC] * 9,
        out_shape=[
            jax.ShapeDtypeStruct((size, cases), F32),
            jax.ShapeDtypeStruct((TROWS, size), BF16),
            jax.ShapeDtypeStruct((TROWS, size), BF16),
            jax.ShapeDtypeStruct((size, 128), BF16),
            jax.ShapeDtypeStruct((size, 128), BF16),
            jax.ShapeDtypeStruct((2, slots, slots), BF16),
            jax.ShapeDtypeStruct((2, slots, slots), BF16),
            jax.ShapeDtypeStruct((ROWS, width), F32),
            jax.ShapeDtypeStruct((lines[0], ROWS + GROUP + span, cases), F32),
        ],
        scratch_shapes=[pltpu.VMEM((128, size), F32), pltpu.VMEM((span, cases), F32)],
        compiler_params=params(12),
        name="frame",
    )(place, modes, free, match, rows, west, north, rhs)


def expansion(lines):
    span = MODES * lines[1]
    out = np.zeros((256, lines[1] * ROWS), np.float32)
    for source in range(lines[1]):
        places = [(0, source), (0, source + 1), (1, source), (0, source - 1), (-1, source)]
        for member, (down, column) in enumerate(places):
            if 0 <= column < lines[1]:
                for mode in range(MODES):
                    at = span * (1 + down) + MODES * column + mode
                    out[at, source * ROWS + member * GROUP + mode] = 1.0
    return jnp.asarray(out, BF16)


def spread_kernel(
    received_ref, expand_ref, operator_ref,
    high_ref, low_ref, a_high_ref, a_low_ref, tail_ref, held_ref, sems,
):
    size = operator_ref.shape[0]
    count = sems.shape[0]
    block = size // count
    copies = []
    for part in range(count):
        rows = pl.ds(part * block, block)
        copies.append(
            pltpu.make_async_copy(operator_ref.at[rows], held_ref.at[rows], sems.at[part])
        )
        copies[-1].start()
    lines, _, cases = received_ref.shape
    tail = TAIL
    tail_ref[...] = jnp.zeros_like(tail_ref)
    packed = received_ref[:, ROWS : ROWS + GROUP, :]
    for member in range(MEMBERS):
        tail_ref[:, member * GROUP : (member + 1) * GROUP, 0:tail] = packed[
            :, :, member * tail : (member + 1) * tail
        ]
    head = split(received_ref[:, 0:ROWS, :].reshape(lines * ROWS, cases))
    rest = split(tail_ref[...].reshape(lines * ROWS, cases))
    for first, last, out in zip(head, rest, (high_ref, low_ref)):
        result = mm(first, expand_ref[0:cases]) + mm(last, expand_ref[cases : 2 * cases])
        out[...] = result.astype(BF16)
    for part in range(count):
        copies[part].wait()
        rows = slice(part * block, (part + 1) * block)
        high, low = split(held_ref[rows, :])
        a_high_ref[rows, :] = high
        a_low_ref[rows, :] = low


def spread(received, expand, operator):
    lines, _, cases = received.shape
    shape = (lines * ROWS, expand.shape[1])
    size = operator.shape[0]
    return pl.pallas_call(
        spread_kernel,
        in_specs=[VMEM_SPEC] * 2 + [pl.BlockSpec(memory_space=pl.ANY)],
        out_specs=[VMEM_SPEC] * 4,
        out_shape=[jax.ShapeDtypeStruct(shape, BF16)] * 2
        + [jax.ShapeDtypeStruct((size, size), BF16)] * 2,
        scratch_shapes=[
            pltpu.VMEM((lines, ROWS, cases), F32), pltpu.VMEM((size, size), F32),
            pltpu.SemaphoreType.DMA((8,)),
        ],
        compiler_params=params(40),
        name="spread",
    )(received, expand, operator)


def solve_kernel(terms_ref, high_ref, low_ref, out_ref):
    terms = terms_ref[...]
    peers, rows, cases = terms.shape
    result = mm3(high_ref[...], low_ref[...], both(terms.reshape(peers * rows, cases)))
    kept = out_ref.shape[1]
    result = result.reshape(out_ref.shape[0], rows, cases)
    total = jnp.sum(terms, axis=0)
    place = lax.broadcasted_iota(jnp.int32, (rows, cases), 0)
    scalar = (place % GROUP) >= MODES
    out_ref[...] = jnp.where(scalar[None], total[None], result)[:, :kept]


def solve(terms, high, low, kept):
    lines = high.shape[0] // ROWS
    return pl.pallas_call(
        solve_kernel,
        in_specs=[VMEM_SPEC] * 3,
        out_specs=VMEM_SPEC,
        out_shape=jax.ShapeDtypeStruct((lines, kept, terms.shape[2]), F32),
        compiler_params=params(8),
        name="solve",
    )(terms, high, low)


def lift(alpha, g_high_ref, g_low_ref):
    filler = jnp.zeros((g_high_ref.shape[1] - alpha.shape[0], alpha.shape[1]), F32)
    pair = both(jnp.concatenate([alpha, filler], axis=0))
    return mm3(g_high_ref[...], g_low_ref[...], pair)


def field_image(r):
    even_x, even_y = r.parity[0] == 0, r.parity[1] == 0
    last_x, last_y = r.parity[2] != 0, r.parity[3] != 0
    slots = r.z_y.shape[1]

    def face(number, own, received):
        mask = r.mask[number * slots : (number + 1) * slots, :]
        return mask * (own + received)

    x_first, x_second = r.x_first[...], r.x_second[...]
    y_first, y_second = r.y_first[...], r.y_second[...]
    result = [
        face(0, r.z_y[0], jnp.where(even_y, y_first, jnp.where(last_y, 0.0, y_second))),
        face(1, r.z_x[0], jnp.where(even_x, x_first, jnp.where(last_x, 0.0, x_second))),
        face(2, r.z_y[1], jnp.where(even_y, y_second, y_first)),
        face(3, r.z_x[1], jnp.where(even_x, x_second, x_first)),
    ]
    return jnp.concatenate(result, axis=0)


def owned_image(r):
    last_x, last_y = r.parity[2] != 0, r.parity[3] != 0
    half = r.mask.shape[0] // 2
    east = r.z_y[0] + jnp.where(last_y, 0.0, r.y_first[...])
    south = r.z_x[0] + jnp.where(last_x, 0.0, r.x_first[...])
    return r.mask[:half, :] * jnp.concatenate([east, south], axis=0)


def member_alpha(total):
    place = lax.broadcasted_iota(jnp.int32, total.shape, 0)
    return jnp.where((place % GROUP) < MODES, total, 0.0)


def apply_faces(r, side, z_ref, first_ref, second_ref, loaded):
    slots = r.gives.shape[1]
    for index in range(2):
        face = side + 2 * index
        rows = slice(face * slots, (face + 1) * slots)
        out = mm3(r.a_high[rows, :], r.a_low[rows, :], r.pair[...])
        if index == 0 and loaded:
            out = out - r.loads[side]
        if index == 1:
            moved = mm(r.gives[side], both(out))
            columns = out.shape[1]
            out = -(moved[:, :columns] + moved[:, columns:])
        z_ref[index] = out
    if second_ref is None:
        first_ref[...] = z_ref[1]
    else:
        flip = r.parity[1 - side]
        first_ref[...] = z_ref[flip]
        second_ref[...] = z_ref[1 - flip]


def update_kernel(phase, names, *refs):
    r = SimpleNamespace(**dict(zip(names, refs)))
    slots = r.gives.shape[1]
    half = 2 * slots
    if phase == 0:
        lines, _, cases = r.received.shape
        span = r.rhs.shape[0] // lines
        for line in range(lines):
            r.rhs[line * span : (line + 1) * span, :] = r.received[line, ROWS + GROUP :]
        alpha = jnp.dot(
            r.coarse[...], r.rhs[...], precision=HIGHEST, preferred_element_type=F32
        )
        field = lift(alpha, r.g_high, r.g_low)
        r.lam_out[...] = field[:half]
    else:
        total = jnp.sum(r.parts[...], axis=0)
        moved = field_image(r) - lift(member_alpha(total), r.g_high, r.g_low)
        if phase == 1:
            field = moved
        elif phase == 2:
            norm = total[NORM_ROW : NORM_ROW + 1, :]
            energy = total[ENERGY_ROW : ENERGY_ROW + 1, :]
            step = norm / energy
            field = r.p[...] + step * moved
            r.q_out[...] = moved
            for place, value in enumerate((norm, energy, step)):
                r.scal_out[place : place + 1, :] = value
        else:
            step, beta, curvature, norm = step_terms(total, r.scal)
            image_p = moved + beta * r.q[...]
            field = r.p[...] + step * image_p
            r.q_out[...] = image_p
            for place, value in enumerate((norm, curvature, step, beta)):
                r.scal_out[place : place + 1, :] = value
        r.p_out[...] = field
    pair = both(field)
    r.pair[:half, :] = pair[:half]
    for side in range(2):
        rows = slice((2 + side) * slots, (3 + side) * slots)
        r.pair[rows, :] = (-mm(r.takes[side], pair[rows])).astype(BF16)
    second = None if phase == LAST else r.send_x_second
    apply_faces(r, 1, r.z_x_out, r.send_x_first, second, phase == 0)


def apply_kernel(phase, names, *refs):
    r = SimpleNamespace(**dict(zip(names, refs)))
    second = None if phase == LAST else r.send_y_second
    apply_faces(r, 0, r.z_y_out, r.send_y_first, second, phase == 0)


def terms_kernel(phase, names, *refs):
    r = SimpleNamespace(**dict(zip(names, refs)))
    slots = r.z_x.shape[1]
    half = 2 * slots
    terms = norm = energy = cross = 0.0
    if phase == 2:
        r.lam_out[...] = r.lam[...] + r.scal[2:3, :] * r.d[:half, :]
    if phase == 3:
        beta = r.scal[3:4, :]
        direction = r.p_old[...] + beta * r.d[...]
        r.d_out[...] = direction
        r.lam_out[...] = r.lam[...] + r.scal[2:3, :] * direction[:half]
    for face in range(4):
        rows = slice(face * slots, (face + 1) * slots)
        own, at = (r.z_x if face % 2 else r.z_y), face // 2
        out = own[at]
        terms = terms + mm3(r.t_high[:, rows], r.t_low[:, rows], both(out))
        if phase >= 1:
            mine = r.p[rows, :]
            energy = energy + jnp.sum(mine * out, axis=0, keepdims=True)
            if face < 2:
                norm = norm + jnp.sum(mine * mine, axis=0, keepdims=True)
        if phase >= 2:
            image = (r.z_x_old if face % 2 else r.z_y_old)[at]
            towards = r.d[rows, :]
            if phase == 3:
                image = image + beta * (r.z_x_older if face % 2 else r.z_y_older)[at]
                towards = r.d_out[rows, :]
            cross = cross + jnp.sum(mine * image + towards * out, axis=0, keepdims=True)
    terms = terms[0:ROWS, :]
    if phase >= 1:
        place = lax.broadcasted_iota(jnp.int32, terms.shape, 0)
        terms = jnp.where(place == NORM_ROW, norm, terms)
        terms = jnp.where(place == ENERGY_ROW, energy, terms)
        if phase >= 2:
            terms = jnp.where(place == CROSS_ROW, cross, terms)
    for peer in range(r.message.shape[0]):
        r.message[peer] = terms


def step_terms(total, scal_ref):
    norm = total[NORM_ROW : NORM_ROW + 1, :]
    energy = total[ENERGY_ROW : ENERGY_ROW + 1, :]
    cross = total[CROSS_ROW : CROSS_ROW + 1, :]
    beta = norm / scal_ref[0:1, :]
    curvature = energy + beta * cross + beta * beta * scal_ref[1:2, :]
    return norm / curvature, beta, curvature, norm


def call(kernel, name, inputs, shapes, scratch=None, halves=(), flops=0):
    scratch = scratch or {}
    keys = list(inputs) + list(shapes) + list(scratch)
    outs = pl.pallas_call(
        functools.partial(kernel, keys),
        in_specs=[VMEM_SPEC if v.shape != (FLAGS,) else SMEM_SPEC for v in inputs.values()],
        out_specs=[VMEM_SPEC] * len(shapes),
        out_shape=[
            jax.ShapeDtypeStruct(shape, BF16 if shape in halves else F32)
            for shape in shapes.values()
        ],
        scratch_shapes=list(scratch.values()),
        compiler_params=params(STEP_MB),
        cost_estimate=pl.CostEstimate(flops=flops, bytes_accessed=4096, transcendentals=0),
        name=name,
    )(*inputs.values())
    return SimpleNamespace(**dict(zip(shapes, outs)))


def step(phase, lines, table, before, exchange, state):
    slots = table.gives.shape[1]
    size = 4 * slots
    cases = table.mask.shape[1]
    face, pair, field = (slots, cases), (2, slots, cases), (size, cases)
    wide = (size, 2 * cases)
    half_flops = size * size * cases * 4
    inputs = dict(
        parity=table.parity, a_high=table.a_high, a_low=table.a_low, gives=table.gives,
        takes=table.takes, g_high=table.g_high, g_low=table.g_low,
    )
    inputs.update(state if before is None else dict(received_by(before), mask=table.mask))
    if phase == 2:
        inputs.update(p=state.p)
    if phase == 3:
        inputs.update(p=state.p, q=state.q, scal=state.scal)
    shapes = dict(pair=wide, z_x_out=pair, send_x_first=face)
    if phase < LAST:
        shapes.update(send_x_second=face)
    scratch = {}
    if phase == 0:
        shapes.update(lam_out=(2 * slots, cases))
        scratch = dict(rhs=pltpu.VMEM((MODES * lines[0] * lines[1], cases), F32))
    else:
        shapes.update(p_out=field)
    if phase >= 2:
        shapes.update(q_out=field, scal_out=(8, cases))
    update = call(
        functools.partial(update_kernel, phase), f"update{phase}", inputs, shapes, scratch,
        (wide,), half_flops,
    )
    inputs = dict(
        parity=table.parity, a_high=table.a_high, a_low=table.a_low, gives=table.gives,
        pair=update.pair,
    )
    if phase == 0:
        inputs.update(loads=state["loads"])
    shapes = dict(z_y_out=pair, send_y_first=face)
    if phase < LAST:
        shapes.update(send_y_second=face)
    apply = call(
        functools.partial(apply_kernel, phase), f"apply{phase}", inputs, shapes, flops=half_flops
    )
    inputs = dict(t_high=table.t_high, t_low=table.t_low, z_x=update.z_x_out, z_y=apply.z_y_out)
    shapes = dict(message=(lines[1], ROWS, cases))
    if phase:
        inputs.update(p=update.p_out)
    if phase >= 2:
        inputs.update(
            scal=update.scal_out, lam=state.lam, d=state.d, z_x_old=before.z_x, z_y_old=before.z_y
        )
        shapes.update(lam_out=(2 * slots, cases))
    if phase == 3:
        inputs.update(p_old=state.p, z_x_older=state.z_x_old, z_y_older=state.z_y_old)
        shapes.update(d_out=field)
    terms = call(
        functools.partial(terms_kernel, phase), f"terms{phase}", inputs, shapes,
        flops=half_flops // 4,
    )
    out = SimpleNamespace(**{**vars(update), **vars(apply), **vars(terms)})
    exchange(out, phase == LAST)
    return out


def received_by(out):
    inputs = dict(parts=out.parts, z_x=out.z_x, z_y=out.z_y, x_first=out.x_first, y_first=out.y_first)
    if out.x_second is not None:
        inputs.update(x_second=out.x_second, y_second=out.y_second)
    return inputs


def final_kernel(names, *refs):
    r = SimpleNamespace(**dict(zip(names, refs)))
    half = r.lam.shape[0]
    top = slice(0, half)
    total = jnp.sum(r.parts[...], axis=0)
    moved = owned_image(r) - lift(
        member_alpha(total), r.g_high.at[top], r.g_low.at[top]
    )
    step_size, beta, _, _ = step_terms(total, r.scal)
    direction = r.p[top, :] + beta * r.d[top, :]
    r.lam_out[...] = r.lam[...] + step_size * direction
    r.p_out[...] = r.p[top, :] + step_size * (moved + beta * r.q[top, :])


def shift(peers, by):
    return [(i, (i + by) % peers) for i in range(peers)]


def swap_first(peers):
    return [(i, i ^ 1) for i in range(peers)]


def swap_second(peers):
    return [(i, (i + (1 if i % 2 else -1)) % peers) for i in range(peers)]


def local(dual_ops, loads, coarse_rhs, coarse_modes, free_mask, face_match, coarse_rows):
    operator = dual_ops[0, 0]
    modes = coarse_modes[0, 0]
    free = free_mask[0, 0]
    rows = coarse_rows[0, 0]
    slots, cases = loads.shape[-2:]
    lines = (lax.axis_size("gx"), lax.axis_size("gy"))
    peers = lines[0] * lines[1]
    at = (lax.axis_index("gx"), lax.axis_index("gy"))
    parity = jnp.stack(
        [
            at[0] % 2, at[1] % 2, at[0] == lines[0] - 1, at[1] == lines[1] - 1,
            at[0] == 0, at[1] == 0,
        ]
    ).astype(jnp.int32)

    pack_east, pack_south, message = pack(rows, modes, free, coarse_rhs[0, 0], lines[1])
    west = lax.ppermute(pack_east, "gy", shift(lines[1], 1))
    north = lax.ppermute(pack_south, "gx", shift(lines[0], 1))
    gathered = lax.all_to_all(message, "gy", 0, 0)
    gathered, west, north, parity = lax.optimization_barrier((gathered, west, north, parity))
    mask, t_high, t_low, g_high, g_low, gives, takes, coarse, pieces = frame(
        lines, parity, modes, free, face_match[0, 0], rows, west, north, gathered
    )
    received = lax.all_to_all(pieces, "gx", 0, 0)
    *solver, a_high, a_low = spread(received, expansion(lines), operator)
    table = SimpleNamespace(
        parity=parity, a_high=a_high, a_low=a_low, mask=mask, t_high=t_high, t_low=t_low,
        g_high=g_high, g_low=g_low, gives=gives, takes=takes,
    )

    def exchange(out, last):
        if last:
            halos = [
                lax.ppermute(out.send_x_first, "gx", shift(lines[0], -1)),
                lax.ppermute(out.send_y_first, "gy", shift(lines[1], -1)),
            ]
        else:
            halos = [
                lax.ppermute(out.send_x_first, "gx", swap_first(lines[0])),
                lax.ppermute(out.send_y_first, "gy", swap_first(lines[1])),
                lax.ppermute(out.send_x_second, "gx", swap_second(lines[0])),
                lax.ppermute(out.send_y_second, "gy", swap_second(lines[1])),
            ]
        terms = lax.all_to_all(out.message, "gy", 0, 0)
        terms, *halos = lax.optimization_barrier((terms, *halos))
        out.x_first, out.y_first = halos[:2]
        out.x_second, out.y_second = (None, None) if last else halos[2:]
        out.parts = lax.all_to_all(solve(terms, *solver, KEPT if last else ROWS), "gx", 0, 0)
        out.z_x, out.z_y = out.z_x_out, out.z_y_out

    run = functools.partial(step, lines=lines, table=table, exchange=exchange)
    start = run(0, before=None, state=dict(received=received, coarse=coarse, loads=loads[0, 0]))
    first = run(1, before=start, state=None)
    second = run(
        2, before=first, state=SimpleNamespace(p=first.p_out, d=first.p_out, lam=start.lam_out)
    )
    third = run(
        3, before=second,
        state=SimpleNamespace(
            p=second.p_out, d=first.p_out, q=second.q_out, scal=second.scal_out,
            lam=second.lam_out, z_x_old=first.z_x, z_y_old=first.z_y,
        ),
    )
    half = (2 * slots, cases)
    out = call(
        final_kernel, "final",
        dict(
            received_by(third), parity=parity, mask=mask, g_high=g_high, g_low=g_low,
            p=third.p_out, d=third.d_out, q=third.q_out, scal=third.scal_out, lam=third.lam_out,
        ),
        dict(lam_out=half, p_out=half),
    )
    shape = (1, 1, 2, slots, cases)
    return out.lam_out.reshape(shape), out.p_out.reshape(shape)


def solution(mesh):
    in_specs = (
        P("gx", "gy", None, None),
        P("gx", "gy", None, None, None),
        P("gx", "gy", None, None),
        P("gx", "gy", None, None, None, None),
        P("gx", "gy", None, None),
        P("gx", "gy", None, None),
        P("gx", "gy", None, None, None),
    )
    out_specs = (P("gx", "gy", None, None, None), P("gx", "gy", None, None, None))
    return jax.shard_map(local, mesh=mesh, in_specs=in_specs, out_specs=out_specs, check_vma=False)
```

```python
import functools
from types import SimpleNamespace

import jax
import jax.numpy as jnp
import numpy as np
from jax import lax
from jax.experimental import pallas as pl
from jax.experimental.pallas import tpu as pltpu
from jax.sharding import PartitionSpec as P

F32 = jnp.float32
BF16 = jnp.bfloat16
HIGHEST = lax.Precision.HIGHEST
MODES = 6
GROUP = 8
MEMBERS = 5
ROWS = GROUP * MEMBERS
TROWS = 48
LAST = 3
FLAGS = 6
KEPT = 3 * GROUP
TAIL = 16
STEP_MB = 16
PACK_MB = 60
NORM_ROW, ENERGY_ROW, CROSS_ROW = 6, 7, 14


VMEM_SPEC = pl.BlockSpec(memory_space=pltpu.VMEM)
SMEM_SPEC = pl.BlockSpec(memory_space=pltpu.SMEM)


def params(megabytes):
    return pltpu.CompilerParams(vmem_limit_bytes=megabytes * 1024 * 1024)


def split(value):
    high = value.astype(BF16)
    low = (value - high.astype(F32)).astype(BF16)
    return high, low


def mm(left, right):
    return jnp.dot(left, right, preferred_element_type=F32)


def both(value):
    high, low = split(value)
    return jnp.concatenate([high, low], axis=1)


def mm3(left_high, left_low, pair):
    columns = pair.shape[1] // 2
    wide = mm(left_high, pair)
    return wide[:, :columns] + wide[:, columns:] + mm(left_low, pair[:, :columns])


def pack_kernel(
    rows_in, modes_in, free_in, match_in, rhs_in,
    east_ref, south_ref, message_ref, own_ref,
    rows_held, modes_held, free_held, match_held, rhs_held, sems,
):
    copies = [
        pltpu.make_async_copy(source, target, sems.at[at])
        for at, (source, target) in enumerate(
            (
                (rows_in, rows_held), (modes_in, modes_held), (free_in, free_held),
                (match_in, match_held), (rhs_in, rhs_held),
            )
        )
    ]
    for copy in copies:
        copy.start()
    for ref in (own_ref, message_ref):
        ref[...] = jnp.zeros_like(ref)
    for copy in copies:
        copy.wait()
    slots = free_held.shape[1]
    for mode in range(MODES):
        for at, member in ((0, 0), (16, 0), (32, 1), (40, 2)):
            own_ref[at + mode : at + mode + 1, :] = rows_held[member, mode]
        for face in range(2):
            at = 16 * face + 8 + mode
            for side in range(2):
                own_ref[at : at + 1, side * slots : (side + 1) * slots] = modes_held[
                    face, mode, side : side + 1, :
                ]
        for peer in range(message_ref.shape[0]):
            message_ref[peer, mode : mode + 1, :] = rhs_held[mode]
    for face in range(2):
        at = 16 * face + MODES
        own_ref[at : at + 1, :slots] = free_held[face : face + 1, :].astype(F32)
        own_ref[at + 1 : at + 2, :slots] = match_held[face : face + 1, :].astype(F32)
    east_ref[...] = own_ref[0:16, :]
    south_ref[...] = own_ref[16:32, :]


def pack(rows, modes, free, match, rhs, peers):
    width = rows.shape[-1]
    cases = rhs.shape[-1]
    rows = rows[:, :, None]
    modes = jnp.swapaxes(modes, 1, 2)
    rhs = rhs[:, None]
    return pl.pallas_call(
        pack_kernel,
        in_specs=[pl.BlockSpec(memory_space=pl.ANY)] * 5,
        out_specs=[VMEM_SPEC] * 4,
        out_shape=[
            jax.ShapeDtypeStruct((16, width), F32),
            jax.ShapeDtypeStruct((16, width), F32),
            jax.ShapeDtypeStruct((peers, GROUP, cases), F32),
            jax.ShapeDtypeStruct((48, width), F32),
        ],
        scratch_shapes=[
            pltpu.VMEM(rows.shape, F32), pltpu.VMEM(modes.shape, F32),
            pltpu.VMEM(free.shape, jnp.int32), pltpu.VMEM(match.shape, jnp.int32),
            pltpu.VMEM(rhs.shape, F32), pltpu.SemaphoreType.DMA((5,)),
        ],
        compiler_params=params(PACK_MB),
        name="pack",
    )(rows, modes, free, match, rhs)


def frame_kernel(
    lines, slots, place_ref, own_ref, west_ref, north_ref, rhs_ref,
    mask_ref, t_high_ref, t_low_ref, g_high_ref, g_low_ref, gives_ref, takes_ref,
    coarse_ref, pieces_ref,
    table_ref, held_ref,
):
    cases = mask_ref.shape[1]
    span = MODES * lines[1]
    modes = [
        own_ref[16 * face + 8 : 16 * face + 8 + MODES, side * slots : (side + 1) * slots]
        for face in range(2)
        for side in range(2)
    ]
    no_north, no_west = place_ref[4] != 0, place_ref[5] != 0
    west = jnp.where(no_west, 0.0, west_ref[...])
    north = jnp.where(no_north, 0.0, north_ref[...])
    table_ref[...] = jnp.zeros_like(table_ref)
    masks = [
        own_ref[6:7, :slots], own_ref[22:23, :slots],
        west[6:7, :slots], north[6:7, :slots],
    ]
    entries = [
        (0, 0, modes[0]), (0, 1, modes[2]),
        (1, 0, modes[1]), (2, 1, modes[3]),
        (3, 2, west[8 : 8 + MODES, :slots]), (0, 2, west[8 : 8 + MODES, slots : 2 * slots]),
        (4, 3, north[8 : 8 + MODES, :slots]), (0, 3, north[8 : 8 + MODES, slots : 2 * slots]),
    ]
    for member, face, values in entries:
        table_ref[member * GROUP : member * GROUP + MODES, face * slots : (face + 1) * slots] = (
            values * masks[face]
        )
    table = table_ref[...]
    high, low = split(table[:TROWS])
    t_high_ref[...] = high
    t_low_ref[...] = low
    high, low = split(table.T)
    g_high_ref[...] = high
    g_low_ref[...] = low
    for face in range(4):
        spread = jnp.broadcast_to(masks[face], (cases, slots))
        mask_ref[face * slots : (face + 1) * slots, :] = spread.T
    order = lax.broadcasted_iota(jnp.int32, (slots, slots), 0).astype(F32)
    for side in range(2):
        moves = jnp.where(order == own_ref[16 * side + 7 : 16 * side + 8, :slots], 1.0, 0.0)
        gives_ref[side] = moves.astype(BF16)
        takes_ref[side] = moves.T.astype(BF16)
    coarse_ref[...] = jnp.zeros_like(coarse_ref)
    members = [own_ref[at : at + MODES, :] for at in (0, 32, 40)]
    members += [west[0:MODES, :], north[0:MODES, :]]
    for member, values in enumerate(members):
        coarse_ref[member * GROUP : member * GROUP + MODES, :] = values
    edge = jnp.zeros((ROWS, span), F32)
    padded = jnp.concatenate([edge, coarse_ref[...], edge], axis=1)
    for source in range(lines[1]):
        held_ref[source * MODES : (source + 1) * MODES, :] = rhs_ref[source, 0:MODES]
    tail = 3 * span - cases
    for line in range(lines[0]):
        first = line * span
        pieces_ref[line, 0:ROWS] = padded[:, first : first + cases]
        last = padded[:, first + cases : first + 3 * span]
        pieces_ref[line, ROWS : ROWS + GROUP] = jnp.zeros((GROUP, cases), F32)
        for member in range(MEMBERS):
            pieces_ref[line, ROWS : ROWS + GROUP, member * tail : (member + 1) * tail] = last[
                member * GROUP : (member + 1) * GROUP
            ]
        pieces_ref[line, ROWS + GROUP :] = held_ref[...]


def frame(lines, slots, place, own, west, north, rhs):
    size = 4 * slots
    width = own.shape[1]
    cases = rhs.shape[-1]
    span = MODES * lines[1]
    return pl.pallas_call(
        functools.partial(frame_kernel, lines, slots),
        in_specs=[SMEM_SPEC] + [VMEM_SPEC] * 4,
        out_specs=[VMEM_SPEC] * 9,
        out_shape=[
            jax.ShapeDtypeStruct((size, cases), F32),
            jax.ShapeDtypeStruct((TROWS, size), BF16),
            jax.ShapeDtypeStruct((TROWS, size), BF16),
            jax.ShapeDtypeStruct((size, 128), BF16),
            jax.ShapeDtypeStruct((size, 128), BF16),
            jax.ShapeDtypeStruct((2, slots, slots), BF16),
            jax.ShapeDtypeStruct((2, slots, slots), BF16),
            jax.ShapeDtypeStruct((ROWS, width), F32),
            jax.ShapeDtypeStruct((lines[0], ROWS + GROUP + span, cases), F32),
        ],
        scratch_shapes=[
            pltpu.VMEM((128, size), F32), pltpu.VMEM((span, cases), F32),
        ],
        compiler_params=params(12),
        name="frame",
    )(place, own, west, north, rhs)


def expansion(lines):
    span = MODES * lines[1]
    out = np.zeros((256, lines[1] * ROWS), np.float32)
    for source in range(lines[1]):
        places = [(0, source), (0, source + 1), (1, source), (0, source - 1), (-1, source)]
        for member, (down, column) in enumerate(places):
            if 0 <= column < lines[1]:
                for mode in range(MODES):
                    at = span * (1 + down) + MODES * column + mode
                    out[at, source * ROWS + member * GROUP + mode] = 1.0
    return jnp.asarray(out, BF16)


def spread_kernel(
    received_ref, expand_in, operator_ref, loads_in,
    high_ref, low_ref, a_high_ref, a_low_ref, loads_ref,
    tail_ref, held_ref, expand_ref, sems, loads_sem, expand_sem,
):
    size = operator_ref.shape[0]
    count = sems.shape[0]
    block = size // count
    expand_copy = pltpu.make_async_copy(expand_in, expand_ref, expand_sem)
    expand_copy.start()
    copies = []
    for part in range(count):
        rows = pl.ds(part * block, block)
        copies.append(
            pltpu.make_async_copy(operator_ref.at[rows], held_ref.at[rows], sems.at[part])
        )
        copies[-1].start()
    loads_copy = pltpu.make_async_copy(loads_in, loads_ref, loads_sem)
    loads_copy.start()
    lines, _, cases = received_ref.shape
    tail = TAIL
    tail_ref[...] = jnp.zeros_like(tail_ref)
    packed = received_ref[:, ROWS : ROWS + GROUP, :]
    for member in range(MEMBERS):
        tail_ref[:, member * GROUP : (member + 1) * GROUP, 0:tail] = packed[
            :, :, member * tail : (member + 1) * tail
        ]
    expand_copy.wait()
    head = split(received_ref[:, 0:ROWS, :].reshape(lines * ROWS, cases))
    rest = split(tail_ref[...].reshape(lines * ROWS, cases))
    for first, last, out in zip(head, rest, (high_ref, low_ref)):
        result = mm(first, expand_ref[0:cases]) + mm(last, expand_ref[cases : 2 * cases])
        out[...] = result.astype(BF16)
    for part in range(count):
        copies[part].wait()
        rows = slice(part * block, (part + 1) * block)
        high, low = split(held_ref[rows, :])
        a_high_ref[rows, :] = high
        a_low_ref[rows, :] = low
    loads_copy.wait()


def spread(received, expand, operator, loads):
    lines, _, cases = received.shape
    shape = (lines * ROWS, expand.shape[1])
    size = operator.shape[0]
    return pl.pallas_call(
        spread_kernel,
        in_specs=[VMEM_SPEC] + [pl.BlockSpec(memory_space=pl.ANY)] * 3,
        out_specs=[VMEM_SPEC] * 5,
        out_shape=[jax.ShapeDtypeStruct(shape, BF16)] * 2
        + [jax.ShapeDtypeStruct((size, size), BF16)] * 2
        + [jax.ShapeDtypeStruct(loads.shape, F32)],
        scratch_shapes=[
            pltpu.VMEM((lines, ROWS, cases), F32), pltpu.VMEM((size, size), F32),
            pltpu.VMEM(expand.shape, BF16),
            pltpu.SemaphoreType.DMA((8,)), pltpu.SemaphoreType.DMA, pltpu.SemaphoreType.DMA,
        ],
        compiler_params=params(40),
        name="spread",
    )(received, expand, operator, loads)


def solve_kernel(terms_ref, high_ref, low_ref, out_ref):
    terms = terms_ref[...]
    peers, rows, cases = terms.shape
    result = mm3(high_ref[...], low_ref[...], both(terms.reshape(peers * rows, cases)))
    kept = out_ref.shape[1]
    result = result.reshape(out_ref.shape[0], rows, cases)
    total = jnp.sum(terms, axis=0)
    place = lax.broadcasted_iota(jnp.int32, (rows, cases), 0)
    scalar = (place % GROUP) >= MODES
    out_ref[...] = jnp.where(scalar[None], total[None], result)[:, :kept]


def solve(terms, high, low, kept):
    lines = high.shape[0] // ROWS
    return pl.pallas_call(
        solve_kernel,
        in_specs=[VMEM_SPEC] * 3,
        out_specs=VMEM_SPEC,
        out_shape=jax.ShapeDtypeStruct((lines, kept, terms.shape[2]), F32),
        compiler_params=params(8),
        name="solve",
    )(terms, high, low)


def lift(alpha, g_high_ref, g_low_ref):
    filler = jnp.zeros((g_high_ref.shape[1] - alpha.shape[0], alpha.shape[1]), F32)
    pair = both(jnp.concatenate([alpha, filler], axis=0))
    return mm3(g_high_ref[...], g_low_ref[...], pair)


def field_image(r):
    even_x, even_y = r.parity[0] == 0, r.parity[1] == 0
    last_x, last_y = r.parity[2] != 0, r.parity[3] != 0
    slots = r.z_y.shape[1]

    def face(number, own, received):
        mask = r.mask[number * slots : (number + 1) * slots, :]
        return mask * (own + received)

    x_first, x_second = r.x_first[...], r.x_second[...]
    y_first, y_second = r.y_first[...], r.y_second[...]
    result = [
        face(0, r.z_y[0], jnp.where(even_y, y_first, jnp.where(last_y, 0.0, y_second))),
        face(1, r.z_x[0], jnp.where(even_x, x_first, jnp.where(last_x, 0.0, x_second))),
        face(2, r.z_y[1], jnp.where(even_y, y_second, y_first)),
        face(3, r.z_x[1], jnp.where(even_x, x_second, x_first)),
    ]
    return jnp.concatenate(result, axis=0)


def owned_image(r):
    last_x, last_y = r.parity[2] != 0, r.parity[3] != 0
    half = r.mask.shape[0] // 2
    east = r.z_y[0] + jnp.where(last_y, 0.0, r.y_first[...])
    south = r.z_x[0] + jnp.where(last_x, 0.0, r.x_first[...])
    return r.mask[:half, :] * jnp.concatenate([east, south], axis=0)


def member_alpha(total):
    place = lax.broadcasted_iota(jnp.int32, total.shape, 0)
    return jnp.where((place % GROUP) < MODES, total, 0.0)


def apply_faces(r, side, z_ref, first_ref, second_ref, loaded):
    slots = r.gives.shape[1]
    for index in (1, 0):
        face = side + 2 * index
        rows = slice(face * slots, (face + 1) * slots)
        out = mm3(r.a_high[rows, :], r.a_low[rows, :], r.pair[...])
        if index == 0 and loaded:
            out = out - r.loads[side]
        if index == 1:
            moved = mm(r.gives[side], both(out))
            columns = out.shape[1]
            out = -(moved[:, :columns] + moved[:, columns:])
        z_ref[index] = out
    if second_ref is None:
        first_ref[...] = z_ref[1]
    else:
        flip = r.parity[1 - side]
        first_ref[...] = z_ref[flip]
        second_ref[...] = z_ref[1 - flip]


def update_kernel(phase, names, *refs):
    r = SimpleNamespace(**dict(zip(names, refs)))
    slots = r.gives.shape[1]
    half = 2 * slots
    if phase == 0:
        lines, _, cases = r.received.shape
        span = r.rhs.shape[0] // lines
        for line in range(lines):
            r.rhs[line * span : (line + 1) * span, :] = r.received[line, ROWS + GROUP :]
        alpha = jnp.dot(
            r.coarse[...], r.rhs[...], precision=HIGHEST, preferred_element_type=F32
        )
        field = lift(alpha, r.g_high, r.g_low)
        r.lam_out[...] = field[:half]
    else:
        total = jnp.sum(r.parts[...], axis=0)
        moved = field_image(r) - lift(member_alpha(total), r.g_high, r.g_low)
        if phase == 1:
            field = moved
        elif phase == 2:
            norm = total[NORM_ROW : NORM_ROW + 1, :]
            energy = total[ENERGY_ROW : ENERGY_ROW + 1, :]
            step = norm / energy
            field = r.p[...] + step * moved
            r.q_out[...] = moved
            for place, value in enumerate((norm, energy, step)):
                r.scal_out[place : place + 1, :] = value
        else:
            step, beta, curvature, norm = step_terms(total, r.scal)
            image_p = moved + beta * r.q[...]
            field = r.p[...] + step * image_p
            r.q_out[...] = image_p
            for place, value in enumerate((norm, curvature, step, beta)):
                r.scal_out[place : place + 1, :] = value
        r.p_out[...] = field
    pair = both(field)
    r.pair[:half, :] = pair[:half]
    for side in range(2):
        rows = slice((2 + side) * slots, (3 + side) * slots)
        r.pair[rows, :] = (-mm(r.takes[side], pair[rows])).astype(BF16)
    second = None if phase == LAST else r.send_x_second
    apply_faces(r, 1, r.z_x_out, r.send_x_first, second, phase == 0)


def apply_kernel(phase, names, *refs):
    r = SimpleNamespace(**dict(zip(names, refs)))
    second = None if phase == LAST else r.send_y_second
    apply_faces(r, 0, r.z_y_out, r.send_y_first, second, phase == 0)


def terms_kernel(phase, names, *refs):
    r = SimpleNamespace(**dict(zip(names, refs)))
    slots = r.z_x.shape[1]
    half = 2 * slots
    terms = norm = energy = cross = 0.0
    if phase == 2:
        r.lam_out[...] = r.lam[...] + r.scal[2:3, :] * r.d[:half, :]
    if phase == 3:
        beta = r.scal[3:4, :]
        direction = r.p_old[...] + beta * r.d[...]
        r.d_out[...] = direction
        r.lam_out[...] = r.lam[...] + r.scal[2:3, :] * direction[:half]
    for face in range(4):
        rows = slice(face * slots, (face + 1) * slots)
        own, at = (r.z_x if face % 2 else r.z_y), face // 2
        out = own[at]
        terms = terms + mm3(r.t_high[:, rows], r.t_low[:, rows], both(out))
        if phase >= 1:
            mine = r.p[rows, :]
            energy = energy + jnp.sum(mine * out, axis=0, keepdims=True)
            if face < 2:
                norm = norm + jnp.sum(mine * mine, axis=0, keepdims=True)
        if phase >= 2:
            image = (r.z_x_old if face % 2 else r.z_y_old)[at]
            towards = r.d[rows, :]
            if phase == 3:
                image = image + beta * (r.z_x_older if face % 2 else r.z_y_older)[at]
                towards = r.d_out[rows, :]
            cross = cross + jnp.sum(mine * image + towards * out, axis=0, keepdims=True)
    terms = terms[0:ROWS, :]
    if phase >= 1:
        place = lax.broadcasted_iota(jnp.int32, terms.shape, 0)
        terms = jnp.where(place == NORM_ROW, norm, terms)
        terms = jnp.where(place == ENERGY_ROW, energy, terms)
        if phase >= 2:
            terms = jnp.where(place == CROSS_ROW, cross, terms)
    for peer in range(r.message.shape[0]):
        r.message[peer] = terms


def step_terms(total, scal_ref):
    norm = total[NORM_ROW : NORM_ROW + 1, :]
    energy = total[ENERGY_ROW : ENERGY_ROW + 1, :]
    cross = total[CROSS_ROW : CROSS_ROW + 1, :]
    beta = norm / scal_ref[0:1, :]
    curvature = energy + beta * cross + beta * beta * scal_ref[1:2, :]
    return norm / curvature, beta, curvature, norm


def call(kernel, name, inputs, shapes, scratch=None, halves=(), flops=0):
    scratch = scratch or {}
    keys = list(inputs) + list(shapes) + list(scratch)
    outs = pl.pallas_call(
        functools.partial(kernel, keys),
        in_specs=[VMEM_SPEC if v.shape != (FLAGS,) else SMEM_SPEC for v in inputs.values()],
        out_specs=[VMEM_SPEC] * len(shapes),
        out_shape=[
            jax.ShapeDtypeStruct(shape, BF16 if shape in halves else F32)
            for shape in shapes.values()
        ],
        scratch_shapes=list(scratch.values()),
        compiler_params=params(STEP_MB),
        cost_estimate=pl.CostEstimate(flops=flops, bytes_accessed=4096, transcendentals=0),
        name=name,
    )(*inputs.values())
    return SimpleNamespace(**dict(zip(shapes, outs)))


def step(phase, lines, table, before, exchange, state):
    slots = table.gives.shape[1]
    size = 4 * slots
    cases = table.mask.shape[1]
    face, pair, field = (slots, cases), (2, slots, cases), (size, cases)
    wide = (size, 2 * cases)
    half_flops = size * size * cases * 4
    inputs = dict(
        parity=table.parity, a_high=table.a_high, a_low=table.a_low, gives=table.gives,
        takes=table.takes, g_high=table.g_high, g_low=table.g_low,
    )
    inputs.update(state if before is None else dict(received_by(before), mask=table.mask))
    if phase == 2:
        inputs.update(p=state.p)
    if phase == 3:
        inputs.update(p=state.p, q=state.q, scal=state.scal)
    shapes = dict(pair=wide, z_x_out=pair, send_x_first=face)
    if phase < LAST:
        shapes.update(send_x_second=face)
    scratch = {}
    if phase == 0:
        shapes.update(lam_out=(2 * slots, cases))
        scratch = dict(rhs=pltpu.VMEM((MODES * lines[0] * lines[1], cases), F32))
    else:
        shapes.update(p_out=field)
    if phase >= 2:
        shapes.update(q_out=field, scal_out=(8, cases))
    update = call(
        functools.partial(update_kernel, phase), f"update{phase}", inputs, shapes, scratch,
        (wide,), half_flops,
    )
    inputs = dict(
        parity=table.parity, a_high=table.a_high, a_low=table.a_low, gives=table.gives,
        pair=update.pair,
    )
    if phase == 0:
        inputs.update(loads=state["loads"])
    shapes = dict(z_y_out=pair, send_y_first=face)
    if phase < LAST:
        shapes.update(send_y_second=face)
    apply = call(
        functools.partial(apply_kernel, phase), f"apply{phase}", inputs, shapes, flops=half_flops
    )
    inputs = dict(t_high=table.t_high, t_low=table.t_low, z_x=update.z_x_out, z_y=apply.z_y_out)
    shapes = dict(message=(lines[1], ROWS, cases))
    if phase:
        inputs.update(p=update.p_out)
    if phase >= 2:
        inputs.update(
            scal=update.scal_out, lam=state.lam, d=state.d, z_x_old=before.z_x, z_y_old=before.z_y
        )
        shapes.update(lam_out=(2 * slots, cases))
    if phase == 3:
        inputs.update(p_old=state.p, z_x_older=state.z_x_old, z_y_older=state.z_y_old)
        shapes.update(d_out=field)
    terms = call(
        functools.partial(terms_kernel, phase), f"terms{phase}", inputs, shapes,
        flops=half_flops // 4,
    )
    out = SimpleNamespace(**{**vars(update), **vars(apply), **vars(terms)})
    exchange(out, phase == LAST)
    return out


def received_by(out):
    inputs = dict(parts=out.parts, z_x=out.z_x, z_y=out.z_y, x_first=out.x_first, y_first=out.y_first)
    if out.x_second is not None:
        inputs.update(x_second=out.x_second, y_second=out.y_second)
    return inputs


def final_kernel(names, *refs):
    r = SimpleNamespace(**dict(zip(names, refs)))
    half = r.lam.shape[0]
    top = slice(0, half)
    total = jnp.sum(r.parts[...], axis=0)
    moved = owned_image(r) - lift(
        member_alpha(total), r.g_high.at[top], r.g_low.at[top]
    )
    step_size, beta, _, _ = step_terms(total, r.scal)
    direction = r.p[top, :] + beta * r.d[top, :]
    r.lam_out[...] = r.lam[...] + step_size * direction
    r.p_out[...] = r.p[top, :] + step_size * (moved + beta * r.q[top, :])


def shift(peers, by):
    return [(i, (i + by) % peers) for i in range(peers)]


def swap_first(peers):
    return [(i, i ^ 1) for i in range(peers)]


def swap_second(peers):
    return [(i, (i + (1 if i % 2 else -1)) % peers) for i in range(peers)]


def local(dual_ops, loads, coarse_rhs, coarse_modes, free_mask, face_match, coarse_rows):
    operator = dual_ops[0, 0]
    slots, cases = loads.shape[-2:]
    lines = (lax.axis_size("gx"), lax.axis_size("gy"))
    peers = lines[0] * lines[1]
    at = (lax.axis_index("gx"), lax.axis_index("gy"))
    parity = jnp.stack(
        [
            at[0] % 2, at[1] % 2, at[0] == lines[0] - 1, at[1] == lines[1] - 1,
            at[0] == 0, at[1] == 0,
        ]
    ).astype(jnp.int32)

    pack_east, pack_south, message, own = pack(
        coarse_rows[0, 0], coarse_modes[0, 0], free_mask[0, 0], face_match[0, 0],
        coarse_rhs[0, 0], lines[1],
    )
    west = lax.ppermute(pack_east, "gy", shift(lines[1], 1))
    north = lax.ppermute(pack_south, "gx", shift(lines[0], 1))
    gathered = lax.all_to_all(message, "gy", 0, 0)
    gathered, west, north, parity = lax.optimization_barrier((gathered, west, north, parity))
    mask, t_high, t_low, g_high, g_low, gives, takes, coarse, pieces = frame(
        lines, slots, parity, own, west, north, gathered
    )
    received = lax.all_to_all(pieces, "gx", 0, 0)
    *solver, a_high, a_low, held_loads = spread(
        received, expansion(lines), operator, loads[0, 0]
    )
    table = SimpleNamespace(
        parity=parity, a_high=a_high, a_low=a_low, mask=mask, t_high=t_high, t_low=t_low,
        g_high=g_high, g_low=g_low, gives=gives, takes=takes,
    )

    def exchange(out, last):
        if last:
            halos = [
                lax.ppermute(out.send_x_first, "gx", shift(lines[0], -1)),
                lax.ppermute(out.send_y_first, "gy", shift(lines[1], -1)),
            ]
        else:
            halos = [
                lax.ppermute(out.send_x_first, "gx", swap_first(lines[0])),
                lax.ppermute(out.send_y_first, "gy", swap_first(lines[1])),
                lax.ppermute(out.send_x_second, "gx", swap_second(lines[0])),
                lax.ppermute(out.send_y_second, "gy", swap_second(lines[1])),
            ]
        terms = lax.all_to_all(out.message, "gy", 0, 0)
        terms, *halos = lax.optimization_barrier((terms, *halos))
        out.x_first, out.y_first = halos[:2]
        out.x_second, out.y_second = (None, None) if last else halos[2:]
        out.parts = lax.all_to_all(solve(terms, *solver, KEPT if last else ROWS), "gx", 0, 0)
        out.z_x, out.z_y = out.z_x_out, out.z_y_out

    run = functools.partial(step, lines=lines, table=table, exchange=exchange)
    start = run(0, before=None, state=dict(received=received, coarse=coarse, loads=held_loads))
    first = run(1, before=start, state=None)
    second = run(
        2, before=first, state=SimpleNamespace(p=first.p_out, d=first.p_out, lam=start.lam_out)
    )
    third = run(
        3, before=second,
        state=SimpleNamespace(
            p=second.p_out, d=first.p_out, q=second.q_out, scal=second.scal_out,
            lam=second.lam_out, z_x_old=first.z_x, z_y_old=first.z_y,
        ),
    )
    half = (2 * slots, cases)
    out = call(
        final_kernel, "final",
        dict(
            received_by(third), parity=parity, mask=mask, g_high=g_high, g_low=g_low,
            p=third.p_out, d=third.d_out, q=third.q_out, scal=third.scal_out, lam=third.lam_out,
        ),
        dict(lam_out=half, p_out=half),
    )
    shape = (1, 1, 2, slots, cases)
    return out.lam_out.reshape(shape), out.p_out.reshape(shape)


def solution(mesh):
    in_specs = (
        P("gx", "gy", None, None),
        P("gx", "gy", None, None, None),
        P("gx", "gy", None, None),
        P("gx", "gy", None, None, None, None),
        P("gx", "gy", None, None),
        P("gx", "gy", None, None),
        P("gx", "gy", None, None, None),
    )
    out_specs = (P("gx", "gy", None, None, None), P("gx", "gy", None, None, None))
    return jax.shard_map(local, mesh=mesh, in_specs=in_specs, out_specs=out_specs, check_vma=False)
```

```python
import functools
from types import SimpleNamespace

import jax
import jax.numpy as jnp
from jax import lax
from jax.experimental import pallas as pl
from jax.experimental.pallas import tpu as pltpu
from jax.sharding import PartitionSpec as P

F32 = jnp.float32
BF16 = jnp.bfloat16
HIGHEST = lax.Precision.HIGHEST
MODES = 6
GROUP = 8
MEMBERS = 5
ROWS = GROUP * MEMBERS
TROWS = 48
LAST = 3
FLAGS = 6
PACKED = 32
KEPT = 3 * GROUP
TAIL = 16
STEP_MB = 16
PACK_MB = 60
NORM_ROW, ENERGY_ROW, CROSS_ROW = 6, 7, 14


VMEM_SPEC = pl.BlockSpec(memory_space=pltpu.VMEM)
SMEM_SPEC = pl.BlockSpec(memory_space=pltpu.SMEM)


def params(megabytes):
    return pltpu.CompilerParams(vmem_limit_bytes=megabytes * 1024 * 1024)


def split(value):
    high = value.astype(BF16)
    low = (value - high.astype(F32)).astype(BF16)
    return high, low


def mm(left, right):
    return jnp.dot(left, right, preferred_element_type=F32)


def both(value):
    high, low = split(value)
    return jnp.concatenate([high, low], axis=1)


def mm3(left_high, left_low, pair):
    columns = pair.shape[1] // 2
    wide = mm(left_high, pair)
    return wide[:, :columns] + wide[:, columns:] + mm(left_low, pair[:, :columns])


def pack_kernel(
    rows_in, modes_in, free_in, match_in, rhs_in,
    east_ref, south_ref, message_ref, own_ref,
    rows_held, modes_held, free_held, match_held, rhs_held, sems,
):
    copies = [
        pltpu.make_async_copy(source, target, sems.at[at])
        for at, (source, target) in enumerate(
            (
                (rows_in, rows_held), (modes_in, modes_held), (free_in, free_held),
                (match_in, match_held), (rhs_in, rhs_held),
            )
        )
    ]
    for copy in copies:
        copy.start()
    for ref in (own_ref, message_ref):
        ref[...] = jnp.zeros_like(ref)
    for copy in copies:
        copy.wait()
    slots = free_held.shape[1]
    for mode in range(MODES):
        for at, member in ((0, 0), (16, 0), (32, 1), (40, 2)):
            own_ref[at + mode : at + mode + 1, :] = rows_held[member, mode]
        for face in range(2):
            at = 16 * face + 8 + mode
            for side in range(2):
                own_ref[at : at + 1, side * slots : (side + 1) * slots] = modes_held[
                    face, mode, side : side + 1, :
                ]
        for peer in range(message_ref.shape[0]):
            message_ref[peer, mode : mode + 1, :] = rhs_held[mode]
    for face in range(2):
        at = 16 * face + MODES
        own_ref[at : at + 1, :slots] = free_held[face : face + 1, :].astype(F32)
        own_ref[at + 1 : at + 2, :slots] = match_held[face : face + 1, :].astype(F32)
    east_ref[...] = own_ref[0:16, :]
    south_ref[...] = own_ref[16:32, :]


def pack(rows, modes, free, match, rhs, peers):
    width = rows.shape[-1]
    cases = rhs.shape[-1]
    rows = rows[:, :, None]
    modes = jnp.swapaxes(modes, 1, 2)
    rhs = rhs[:, None]
    return pl.pallas_call(
        pack_kernel,
        in_specs=[pl.BlockSpec(memory_space=pl.ANY)] * 5,
        out_specs=[VMEM_SPEC] * 4,
        out_shape=[
            jax.ShapeDtypeStruct((16, width), F32),
            jax.ShapeDtypeStruct((16, width), F32),
            jax.ShapeDtypeStruct((peers, GROUP, cases), F32),
            jax.ShapeDtypeStruct((48, width), F32),
        ],
        scratch_shapes=[
            pltpu.VMEM(rows.shape, F32), pltpu.VMEM(modes.shape, F32),
            pltpu.VMEM(free.shape, jnp.int32), pltpu.VMEM(match.shape, jnp.int32),
            pltpu.VMEM(rhs.shape, F32), pltpu.SemaphoreType.DMA((5,)),
        ],
        compiler_params=params(PACK_MB),
        name="pack",
    )(rows, modes, free, match, rhs)


def frame_kernel(
    lines, slots, place_ref, own_ref, west_ref, north_ref, rhs_ref,
    mask_ref, t_high_ref, t_low_ref, g_high_ref, g_low_ref, gives_ref, takes_ref,
    coarse_ref, pieces_ref,
    table_ref, held_ref,
):
    cases = mask_ref.shape[1]
    span = MODES * lines[1]
    modes = [
        own_ref[16 * face + 8 : 16 * face + 8 + MODES, side * slots : (side + 1) * slots]
        for face in range(2)
        for side in range(2)
    ]
    no_north, no_west = place_ref[4] != 0, place_ref[5] != 0
    west = jnp.where(no_west, 0.0, west_ref[...])
    north = jnp.where(no_north, 0.0, north_ref[...])
    table_ref[...] = jnp.zeros_like(table_ref)
    masks = [
        own_ref[6:7, :slots], own_ref[22:23, :slots],
        west[6:7, :slots], north[6:7, :slots],
    ]
    entries = [
        (0, 0, modes[0]), (0, 1, modes[2]),
        (1, 0, modes[1]), (2, 1, modes[3]),
        (3, 2, west[8 : 8 + MODES, :slots]), (0, 2, west[8 : 8 + MODES, slots : 2 * slots]),
        (4, 3, north[8 : 8 + MODES, :slots]), (0, 3, north[8 : 8 + MODES, slots : 2 * slots]),
    ]
    for member, face, values in entries:
        table_ref[member * GROUP : member * GROUP + MODES, face * slots : (face + 1) * slots] = (
            values * masks[face]
        )
    table = table_ref[...]
    high, low = split(table[:TROWS])
    t_high_ref[...] = high
    t_low_ref[...] = low
    high, low = split(table.T)
    g_high_ref[...] = high
    g_low_ref[...] = low
    for face in range(4):
        spread = jnp.broadcast_to(masks[face], (cases, slots))
        mask_ref[face * slots : (face + 1) * slots, :] = spread.T
    order = lax.broadcasted_iota(jnp.int32, (slots, slots), 0).astype(F32)
    for side in range(2):
        moves = jnp.where(order == own_ref[16 * side + 7 : 16 * side + 8, :slots], 1.0, 0.0)
        gives_ref[side] = moves.astype(BF16)
        takes_ref[side] = moves.T.astype(BF16)
    coarse_ref[...] = jnp.zeros_like(coarse_ref)
    members = [own_ref[at : at + MODES, :] for at in (0, 32, 40)]
    members += [west[0:MODES, :], north[0:MODES, :]]
    for member, values in enumerate(members):
        coarse_ref[member * GROUP : member * GROUP + MODES, :] = values
    edge = jnp.zeros((ROWS, span), F32)
    padded = jnp.concatenate([edge, coarse_ref[...], edge], axis=1)
    for source in range(lines[1]):
        held_ref[source * MODES : (source + 1) * MODES, :] = rhs_ref[source, 0:MODES]
    tail = 3 * span - cases
    for line in range(lines[0]):
        first = line * span
        pieces_ref[line, 0:ROWS] = padded[:, first : first + cases]
        last = padded[:, first + cases : first + 3 * span]
        pieces_ref[line, ROWS : ROWS + GROUP] = jnp.zeros((GROUP, cases), F32)
        for member in range(MEMBERS):
            pieces_ref[line, ROWS : ROWS + GROUP, member * tail : (member + 1) * tail] = last[
                member * GROUP : (member + 1) * GROUP
            ]
        pieces_ref[line, ROWS + GROUP :] = held_ref[...]


def frame(lines, slots, place, own, west, north, rhs):
    size = 4 * slots
    width = own.shape[1]
    cases = rhs.shape[-1]
    span = MODES * lines[1]
    return pl.pallas_call(
        functools.partial(frame_kernel, lines, slots),
        in_specs=[SMEM_SPEC] + [VMEM_SPEC] * 4,
        out_specs=[VMEM_SPEC] * 9,
        out_shape=[
            jax.ShapeDtypeStruct((size, cases), F32),
            jax.ShapeDtypeStruct((TROWS, size), BF16),
            jax.ShapeDtypeStruct((TROWS, size), BF16),
            jax.ShapeDtypeStruct((size, 128), BF16),
            jax.ShapeDtypeStruct((size, 128), BF16),
            jax.ShapeDtypeStruct((2, slots, slots), BF16),
            jax.ShapeDtypeStruct((2, slots, slots), BF16),
            jax.ShapeDtypeStruct((ROWS, width), F32),
            jax.ShapeDtypeStruct((lines[0], ROWS + GROUP + span, cases), F32),
        ],
        scratch_shapes=[
            pltpu.VMEM((128, size), F32), pltpu.VMEM((span, cases), F32),
        ],
        compiler_params=params(12),
        name="frame",
    )(place, own, west, north, rhs)


def expansion(table_ref, columns):
    span = MODES * columns
    table_ref[...] = jnp.zeros_like(table_ref)
    row = lax.broadcasted_iota(jnp.int32, (MODES, MODES), 0)
    one = jnp.where(row == lax.broadcasted_iota(jnp.int32, (MODES, MODES), 1), 1.0, 0.0)
    for source in range(columns):
        places = [(0, source), (0, source + 1), (1, source), (0, source - 1), (-1, source)]
        for member, (down, column) in enumerate(places):
            if 0 <= column < columns:
                to = span * (1 + down) + MODES * column
                at = source * ROWS + member * GROUP
                table_ref[to : to + MODES, at : at + MODES] = one


def spread_kernel(
    received_ref, operator_ref, loads_in,
    high_ref, low_ref, a_high_ref, a_low_ref, loads_ref,
    tail_ref, held_ref, expand_ref, sems, loads_sem,
):
    size = operator_ref.shape[0]
    count = sems.shape[0]
    block = size // count
    copies = []
    for part in range(count):
        rows = pl.ds(part * block, block)
        copies.append(
            pltpu.make_async_copy(operator_ref.at[rows], held_ref.at[rows], sems.at[part])
        )
        copies[-1].start()
    loads_copy = pltpu.make_async_copy(loads_in, loads_ref, loads_sem)
    loads_copy.start()
    lines, _, cases = received_ref.shape
    tail = TAIL
    tail_ref[...] = jnp.zeros_like(tail_ref)
    packed = received_ref[:, ROWS : ROWS + GROUP, :]
    for member in range(MEMBERS):
        tail_ref[:, member * GROUP : (member + 1) * GROUP, 0:tail] = packed[
            :, :, member * tail : (member + 1) * tail
        ]
    expansion(expand_ref, expand_ref.shape[1] // ROWS)
    expand = expand_ref[...].astype(BF16)
    head = split(received_ref[:, 0:ROWS, :].reshape(lines * ROWS, cases))
    rest = split(tail_ref[...].reshape(lines * ROWS, cases))
    for first, last, out in zip(head, rest, (high_ref, low_ref)):
        result = mm(first, expand[0:cases]) + mm(last, expand[cases : 2 * cases])
        out[...] = result.astype(BF16)
    for part in range(count):
        copies[part].wait()
        rows = slice(part * block, (part + 1) * block)
        high, low = split(held_ref[rows, :])
        a_high_ref[rows, :] = high
        a_low_ref[rows, :] = low
    loads_copy.wait()


def spread(received, columns, operator, loads):
    lines, _, cases = received.shape
    shape = (lines * ROWS, columns * ROWS)
    size = operator.shape[0]
    return pl.pallas_call(
        spread_kernel,
        in_specs=[VMEM_SPEC] + [pl.BlockSpec(memory_space=pl.ANY)] * 2,
        out_specs=[VMEM_SPEC] * 5,
        out_shape=[jax.ShapeDtypeStruct(shape, BF16)] * 2
        + [jax.ShapeDtypeStruct((size, size), BF16)] * 2
        + [jax.ShapeDtypeStruct(loads.shape, F32)],
        scratch_shapes=[
            pltpu.VMEM((lines, ROWS, cases), F32), pltpu.VMEM((size, size), F32),
            pltpu.VMEM((2 * cases, columns * ROWS), F32),
            pltpu.SemaphoreType.DMA((8,)), pltpu.SemaphoreType.DMA,
        ],
        compiler_params=params(40),
        name="spread",
    )(received, operator, loads)


def solve_kernel(terms_ref, high_ref, low_ref, out_ref):
    terms = terms_ref[...]
    peers, rows, cases = terms.shape
    result = mm3(high_ref[...], low_ref[...], both(terms.reshape(peers * rows, cases)))
    kept = out_ref.shape[1]
    result = result.reshape(out_ref.shape[0], rows, cases)
    total = jnp.sum(terms, axis=0)
    place = lax.broadcasted_iota(jnp.int32, (rows, cases), 0)
    scalar = (place % GROUP) >= MODES
    if kept == PACKED:
        for member in range(MEMBERS):
            out_ref[:, member * MODES : (member + 1) * MODES, :] = result[
                :, member * GROUP : member * GROUP + MODES
            ]
        sums = total[MODES:GROUP]
        out_ref[:, MEMBERS * MODES : PACKED, :] = jnp.broadcast_to(
            sums[None], (out_ref.shape[0],) + sums.shape
        )
    else:
        out_ref[...] = jnp.where(scalar[None], total[None], result)[:, :kept]


def solve(terms, high, low, kept):
    lines = high.shape[0] // ROWS
    return pl.pallas_call(
        solve_kernel,
        in_specs=[VMEM_SPEC] * 3,
        out_specs=VMEM_SPEC,
        out_shape=jax.ShapeDtypeStruct((lines, kept, terms.shape[2]), F32),
        compiler_params=params(8),
        name="solve",
    )(terms, high, low)


def lift(alpha, g_high_ref, g_low_ref):
    filler = jnp.zeros((g_high_ref.shape[1] - alpha.shape[0], alpha.shape[1]), F32)
    pair = both(jnp.concatenate([alpha, filler], axis=0))
    return mm3(g_high_ref[...], g_low_ref[...], pair)


def field_image(r):
    even_x, even_y = r.parity[0] == 0, r.parity[1] == 0
    last_x, last_y = r.parity[2] != 0, r.parity[3] != 0
    slots = r.z_y.shape[1]

    def face(number, own, received):
        mask = r.mask[number * slots : (number + 1) * slots, :]
        return mask * (own + received)

    x_first, x_second = r.x_first[...], r.x_second[...]
    y_first, y_second = r.y_first[...], r.y_second[...]
    result = [
        face(0, r.z_y[0], jnp.where(even_y, y_first, jnp.where(last_y, 0.0, y_second))),
        face(1, r.z_x[0], jnp.where(even_x, x_first, jnp.where(last_x, 0.0, x_second))),
        face(2, r.z_y[1], jnp.where(even_y, y_second, y_first)),
        face(3, r.z_x[1], jnp.where(even_x, x_second, x_first)),
    ]
    return jnp.concatenate(result, axis=0)


def owned_image(r):
    last_x, last_y = r.parity[2] != 0, r.parity[3] != 0
    half = r.mask.shape[0] // 2
    east = r.z_y[0] + jnp.where(last_y, 0.0, r.y_first[...])
    south = r.z_x[0] + jnp.where(last_x, 0.0, r.x_first[...])
    return r.mask[:half, :] * jnp.concatenate([east, south], axis=0)


def member_alpha(total):
    place = lax.broadcasted_iota(jnp.int32, total.shape, 0)
    return jnp.where((place % GROUP) < MODES, total, 0.0)


def apply_faces(r, side, z_ref, first_ref, second_ref, loaded):
    slots = r.gives.shape[1]
    for index in (1, 0):
        face = side + 2 * index
        rows = slice(face * slots, (face + 1) * slots)
        out = mm3(r.a_high[rows, :], r.a_low[rows, :], r.pair[...])
        if index == 0 and loaded:
            out = out - r.loads[side]
        if index == 1:
            moved = mm(r.gives[side], both(out))
            columns = out.shape[1]
            out = -(moved[:, :columns] + moved[:, columns:])
        z_ref[index] = out
    if second_ref is None:
        first_ref[...] = z_ref[1]
    else:
        flip = r.parity[1 - side]
        first_ref[...] = z_ref[flip]
        second_ref[...] = z_ref[1 - flip]


def update_kernel(phase, names, *refs):
    r = SimpleNamespace(**dict(zip(names, refs)))
    slots = r.gives.shape[1]
    half = 2 * slots
    if phase == 0:
        lines, _, cases = r.received.shape
        span = r.rhs.shape[0] // lines
        for line in range(lines):
            r.rhs[line * span : (line + 1) * span, :] = r.received[line, ROWS + GROUP :]
        alpha = jnp.dot(
            r.coarse[...], r.rhs[...], precision=HIGHEST, preferred_element_type=F32
        )
        field = lift(alpha, r.g_high, r.g_low)
        r.lam_out[...] = field[:half]
    else:
        total = jnp.sum(r.parts[...], axis=0)
        if total.shape[0] == PACKED:
            for member in range(MEMBERS):
                at = member * GROUP
                r.grouped[at : at + MODES, :] = total[member * MODES : (member + 1) * MODES]
                r.grouped[at + MODES : at + GROUP, :] = total[MEMBERS * MODES : PACKED]
            total = r.grouped[...]
        moved = field_image(r) - lift(member_alpha(total), r.g_high, r.g_low)
        if phase == 1:
            field = moved
        elif phase == 2:
            norm = total[NORM_ROW : NORM_ROW + 1, :]
            energy = total[ENERGY_ROW : ENERGY_ROW + 1, :]
            step = norm / energy
            field = r.p[...] + step * moved
            r.q_out[...] = moved
            for place, value in enumerate((norm, energy, step)):
                r.scal_out[place : place + 1, :] = value
        else:
            step, beta, curvature, norm = step_terms(total, r.scal)
            image_p = moved + beta * r.q[...]
            field = r.p[...] + step * image_p
            r.q_out[...] = image_p
            for place, value in enumerate((norm, curvature, step, beta)):
                r.scal_out[place : place + 1, :] = value
        r.p_out[...] = field
    pair = both(field)
    r.pair[:half, :] = pair[:half]
    for side in range(2):
        rows = slice((2 + side) * slots, (3 + side) * slots)
        r.pair[rows, :] = (-mm(r.takes[side], pair[rows])).astype(BF16)
    second = None if phase == LAST else r.send_x_second
    apply_faces(r, 1, r.z_x_out, r.send_x_first, second, phase == 0)


def apply_kernel(phase, names, *refs):
    r = SimpleNamespace(**dict(zip(names, refs)))
    second = None if phase == LAST else r.send_y_second
    apply_faces(r, 0, r.z_y_out, r.send_y_first, second, phase == 0)


def terms_kernel(phase, names, *refs):
    r = SimpleNamespace(**dict(zip(names, refs)))
    slots = r.z_x.shape[1]
    half = 2 * slots
    terms = norm = energy = cross = 0.0
    if phase == 2:
        r.lam_out[...] = r.lam[...] + r.scal[2:3, :] * r.d[:half, :]
    if phase == 3:
        beta = r.scal[3:4, :]
        direction = r.p_old[...] + beta * r.d[...]
        r.d_out[...] = direction
        r.lam_out[...] = r.lam[...] + r.scal[2:3, :] * direction[:half]
    for face in range(4):
        rows = slice(face * slots, (face + 1) * slots)
        own, at = (r.z_x if face % 2 else r.z_y), face // 2
        out = own[at]
        terms = terms + mm3(r.t_high[:, rows], r.t_low[:, rows], both(out))
        if phase >= 1:
            mine = r.p[rows, :]
            energy = energy + jnp.sum(mine * out, axis=0, keepdims=True)
            if face < 2:
                norm = norm + jnp.sum(mine * mine, axis=0, keepdims=True)
        if phase >= 2:
            image = (r.z_x_old if face % 2 else r.z_y_old)[at]
            towards = r.d[rows, :]
            if phase == 3:
                image = image + beta * (r.z_x_older if face % 2 else r.z_y_older)[at]
                towards = r.d_out[rows, :]
            cross = cross + jnp.sum(mine * image + towards * out, axis=0, keepdims=True)
    terms = terms[0:ROWS, :]
    if phase >= 1:
        place = lax.broadcasted_iota(jnp.int32, terms.shape, 0)
        terms = jnp.where(place == NORM_ROW, norm, terms)
        terms = jnp.where(place == ENERGY_ROW, energy, terms)
        if phase >= 2:
            terms = jnp.where(place == CROSS_ROW, cross, terms)
    for peer in range(r.message.shape[0]):
        r.message[peer] = terms


def step_terms(total, scal_ref):
    norm = total[NORM_ROW : NORM_ROW + 1, :]
    energy = total[ENERGY_ROW : ENERGY_ROW + 1, :]
    cross = total[CROSS_ROW : CROSS_ROW + 1, :]
    beta = norm / scal_ref[0:1, :]
    curvature = energy + beta * cross + beta * beta * scal_ref[1:2, :]
    return norm / curvature, beta, curvature, norm


def call(kernel, name, inputs, shapes, scratch=None, halves=(), flops=0):
    scratch = scratch or {}
    keys = list(inputs) + list(shapes) + list(scratch)
    outs = pl.pallas_call(
        functools.partial(kernel, keys),
        in_specs=[VMEM_SPEC if v.shape != (FLAGS,) else SMEM_SPEC for v in inputs.values()],
        out_specs=[VMEM_SPEC] * len(shapes),
        out_shape=[
            jax.ShapeDtypeStruct(shape, BF16 if shape in halves else F32)
            for shape in shapes.values()
        ],
        scratch_shapes=list(scratch.values()),
        compiler_params=params(STEP_MB),
        cost_estimate=pl.CostEstimate(flops=flops, bytes_accessed=4096, transcendentals=0),
        name=name,
    )(*inputs.values())
    return SimpleNamespace(**dict(zip(shapes, outs)))


def step(phase, lines, table, before, exchange, state):
    slots = table.gives.shape[1]
    size = 4 * slots
    cases = table.mask.shape[1]
    face, pair, field = (slots, cases), (2, slots, cases), (size, cases)
    wide = (size, 2 * cases)
    half_flops = size * size * cases * 4
    inputs = dict(
        parity=table.parity, a_high=table.a_high, a_low=table.a_low, gives=table.gives,
        takes=table.takes, g_high=table.g_high, g_low=table.g_low,
    )
    inputs.update(state if before is None else dict(received_by(before), mask=table.mask))
    if phase == 2:
        inputs.update(p=state.p)
    if phase == 3:
        inputs.update(p=state.p, q=state.q, scal=state.scal)
    shapes = dict(pair=wide, z_x_out=pair, send_x_first=face)
    if phase < LAST:
        shapes.update(send_x_second=face)
    scratch = {}
    if phase == 0:
        shapes.update(lam_out=(2 * slots, cases))
        scratch = dict(rhs=pltpu.VMEM((MODES * lines[0] * lines[1], cases), F32))
    else:
        shapes.update(p_out=field)
        scratch = dict(grouped=pltpu.VMEM((ROWS, cases), F32))
    if phase >= 2:
        shapes.update(q_out=field, scal_out=(8, cases))
    update = call(
        functools.partial(update_kernel, phase), f"update{phase}", inputs, shapes, scratch,
        (wide,), half_flops,
    )
    inputs = dict(
        parity=table.parity, a_high=table.a_high, a_low=table.a_low, gives=table.gives,
        pair=update.pair,
    )
    if phase == 0:
        inputs.update(loads=state["loads"])
    shapes = dict(z_y_out=pair, send_y_first=face)
    if phase < LAST:
        shapes.update(send_y_second=face)
    apply = call(
        functools.partial(apply_kernel, phase), f"apply{phase}", inputs, shapes, flops=half_flops
    )
    inputs = dict(t_high=table.t_high, t_low=table.t_low, z_x=update.z_x_out, z_y=apply.z_y_out)
    shapes = dict(message=(lines[1], ROWS, cases))
    if phase:
        inputs.update(p=update.p_out)
    if phase >= 2:
        inputs.update(
            scal=update.scal_out, lam=state.lam, d=state.d, z_x_old=before.z_x, z_y_old=before.z_y
        )
        shapes.update(lam_out=(2 * slots, cases))
    if phase == 3:
        inputs.update(p_old=state.p, z_x_older=state.z_x_old, z_y_older=state.z_y_old)
        shapes.update(d_out=field)
    terms = call(
        functools.partial(terms_kernel, phase), f"terms{phase}", inputs, shapes,
        flops=half_flops // 4,
    )
    out = SimpleNamespace(**{**vars(update), **vars(apply), **vars(terms)})
    exchange(out, phase)
    return out


def received_by(out):
    inputs = dict(parts=out.parts, z_x=out.z_x, z_y=out.z_y, x_first=out.x_first, y_first=out.y_first)
    if out.x_second is not None:
        inputs.update(x_second=out.x_second, y_second=out.y_second)
    return inputs


def final_kernel(names, *refs):
    r = SimpleNamespace(**dict(zip(names, refs)))
    half = r.lam.shape[0]
    top = slice(0, half)
    total = jnp.sum(r.parts[...], axis=0)
    moved = owned_image(r) - lift(
        member_alpha(total), r.g_high.at[top], r.g_low.at[top]
    )
    step_size, beta, _, _ = step_terms(total, r.scal)
    direction = r.p[top, :] + beta * r.d[top, :]
    r.lam_out[...] = r.lam[...] + step_size * direction
    r.p_out[...] = r.p[top, :] + step_size * (moved + beta * r.q[top, :])


def shift(peers, by):
    return [(i, (i + by) % peers) for i in range(peers)]


def swap_first(peers):
    return [(i, i ^ 1) for i in range(peers)]


def swap_second(peers):
    return [(i, (i + (1 if i % 2 else -1)) % peers) for i in range(peers)]


def local(dual_ops, loads, coarse_rhs, coarse_modes, free_mask, face_match, coarse_rows):
    operator = dual_ops[0, 0]
    slots, cases = loads.shape[-2:]
    lines = (lax.axis_size("gx"), lax.axis_size("gy"))
    peers = lines[0] * lines[1]
    at = (lax.axis_index("gx"), lax.axis_index("gy"))
    parity = jnp.stack(
        [
            at[0] % 2, at[1] % 2, at[0] == lines[0] - 1, at[1] == lines[1] - 1,
            at[0] == 0, at[1] == 0,
        ]
    ).astype(jnp.int32)

    pack_east, pack_south, message, own = pack(
        coarse_rows[0, 0], coarse_modes[0, 0], free_mask[0, 0], face_match[0, 0],
        coarse_rhs[0, 0], lines[1],
    )
    west = lax.ppermute(pack_east, "gy", shift(lines[1], 1))
    north = lax.ppermute(pack_south, "gx", shift(lines[0], 1))
    gathered = lax.all_to_all(message, "gy", 0, 0)
    gathered, west, north, parity = lax.optimization_barrier((gathered, west, north, parity))
    mask, t_high, t_low, g_high, g_low, gives, takes, coarse, pieces = frame(
        lines, slots, parity, own, west, north, gathered
    )
    received = lax.all_to_all(pieces, "gx", 0, 0)
    *solver, a_high, a_low, held_loads = spread(
        received, lines[1], operator, loads[0, 0]
    )
    table = SimpleNamespace(
        parity=parity, a_high=a_high, a_low=a_low, mask=mask, t_high=t_high, t_low=t_low,
        g_high=g_high, g_low=g_low, gives=gives, takes=takes,
    )

    def exchange(out, phase):
        last = phase == LAST
        kept = {0: PACKED, 1: PACKED, LAST: KEPT}.get(phase, ROWS)
        if last:
            halos = [
                lax.ppermute(out.send_x_first, "gx", shift(lines[0], -1)),
                lax.ppermute(out.send_y_first, "gy", shift(lines[1], -1)),
            ]
        else:
            halos = [
                lax.ppermute(out.send_x_first, "gx", swap_first(lines[0])),
                lax.ppermute(out.send_y_first, "gy", swap_first(lines[1])),
                lax.ppermute(out.send_x_second, "gx", swap_second(lines[0])),
                lax.ppermute(out.send_y_second, "gy", swap_second(lines[1])),
            ]
        terms = lax.all_to_all(out.message, "gy", 0, 0)
        terms, *halos = lax.optimization_barrier((terms, *halos))
        out.x_first, out.y_first = halos[:2]
        out.x_second, out.y_second = (None, None) if last else halos[2:]
        out.parts = lax.all_to_all(solve(terms, *solver, kept), "gx", 0, 0)
        out.z_x, out.z_y = out.z_x_out, out.z_y_out

    run = functools.partial(step, lines=lines, table=table, exchange=exchange)
    start = run(0, before=None, state=dict(received=received, coarse=coarse, loads=held_loads))
    first = run(1, before=start, state=None)
    second = run(
        2, before=first, state=SimpleNamespace(p=first.p_out, d=first.p_out, lam=start.lam_out)
    )
    third = run(
        3, before=second,
        state=SimpleNamespace(
            p=second.p_out, d=first.p_out, q=second.q_out, scal=second.scal_out,
            lam=second.lam_out, z_x_old=first.z_x, z_y_old=first.z_y,
        ),
    )
    half = (2 * slots, cases)
    out = call(
        final_kernel, "final",
        dict(
            received_by(third), parity=parity, mask=mask, g_high=g_high, g_low=g_low,
            p=third.p_out, d=third.d_out, q=third.q_out, scal=third.scal_out, lam=third.lam_out,
        ),
        dict(lam_out=half, p_out=half),
    )
    shape = (1, 1, 2, slots, cases)
    return out.lam_out.reshape(shape), out.p_out.reshape(shape)


def solution(mesh):
    in_specs = (
        P("gx", "gy", None, None),
        P("gx", "gy", None, None, None),
        P("gx", "gy", None, None),
        P("gx", "gy", None, None, None, None),
        P("gx", "gy", None, None),
        P("gx", "gy", None, None),
        P("gx", "gy", None, None, None),
    )
    out_specs = (P("gx", "gy", None, None, None), P("gx", "gy", None, None, None))
    return jax.shard_map(local, mesh=mesh, in_specs=in_specs, out_specs=out_specs, check_vma=False)
```

```python
import functools
from types import SimpleNamespace

import jax
import jax.numpy as jnp
from jax import lax
from jax.experimental import pallas as pl
from jax.experimental.pallas import tpu as pltpu
from jax.sharding import PartitionSpec as P

F32 = jnp.float32
BF16 = jnp.bfloat16
HIGHEST = lax.Precision.HIGHEST
MODES = 6
GROUP = 8
MEMBERS = 5
ROWS = GROUP * MEMBERS
TROWS = 48
LAST = 3
FLAGS = 6
PACKED = 32
KEPT = 3 * GROUP
TAIL = 16
STEP_MB = 16
PACK_MB = 60
NORM_ROW, ENERGY_ROW, CROSS_ROW = 6, 7, 14


VMEM_SPEC = pl.BlockSpec(memory_space=pltpu.VMEM)
SMEM_SPEC = pl.BlockSpec(memory_space=pltpu.SMEM)


def params(megabytes):
    return pltpu.CompilerParams(vmem_limit_bytes=megabytes * 1024 * 1024)


def split(value):
    high = value.astype(BF16)
    low = (value - high.astype(F32)).astype(BF16)
    return high, low


def mm(left, right):
    return jnp.dot(left, right, preferred_element_type=F32)


def both(value):
    high, low = split(value)
    return jnp.concatenate([high, low], axis=1)


def mm3(left_high, left_low, pair):
    columns = pair.shape[1] // 2
    wide = mm(left_high, pair)
    return wide[:, :columns] + wide[:, columns:] + mm(left_low, pair[:, :columns])


def pack_kernel(
    rows_in, modes_in, free_in, match_in, rhs_in,
    east_ref, south_ref, message_ref, own_ref,
    rows_held, modes_held, free_held, match_held, rhs_held, sems,
):
    copies = [
        pltpu.make_async_copy(source, target, sems.at[at])
        for at, (source, target) in enumerate(
            (
                (rows_in, rows_held), (modes_in, modes_held), (free_in, free_held),
                (match_in, match_held), (rhs_in, rhs_held),
            )
        )
    ]
    for copy in copies:
        copy.start()
    for ref in (own_ref, message_ref):
        ref[...] = jnp.zeros_like(ref)
    for copy in copies:
        copy.wait()
    slots = free_held.shape[1]
    for mode in range(MODES):
        for at, member in ((0, 0), (16, 0), (32, 1), (40, 2)):
            own_ref[at + mode : at + mode + 1, :] = rows_held[member, mode]
        for face in range(2):
            at = 16 * face + 8 + mode
            for side in range(2):
                own_ref[at : at + 1, side * slots : (side + 1) * slots] = modes_held[
                    face, mode, side : side + 1, :
                ]
        for peer in range(message_ref.shape[0]):
            message_ref[peer, mode : mode + 1, :] = rhs_held[mode]
    for face in range(2):
        at = 16 * face + MODES
        own_ref[at : at + 1, :slots] = free_held[face : face + 1, :].astype(F32)
        own_ref[at + 1 : at + 2, :slots] = match_held[face : face + 1, :].astype(F32)
    east_ref[...] = own_ref[0:16, :]
    south_ref[...] = own_ref[16:32, :]


def pack(rows, modes, free, match, rhs, peers):
    width = rows.shape[-1]
    cases = rhs.shape[-1]
    rows = rows[:, :, None]
    modes = jnp.swapaxes(modes, 1, 2)
    rhs = rhs[:, None]
    return pl.pallas_call(
        pack_kernel,
        in_specs=[pl.BlockSpec(memory_space=pl.ANY)] * 5,
        out_specs=[VMEM_SPEC] * 4,
        out_shape=[
            jax.ShapeDtypeStruct((16, width), F32),
            jax.ShapeDtypeStruct((16, width), F32),
            jax.ShapeDtypeStruct((peers, GROUP, cases), F32),
            jax.ShapeDtypeStruct((48, width), F32),
        ],
        scratch_shapes=[
            pltpu.VMEM(rows.shape, F32), pltpu.VMEM(modes.shape, F32),
            pltpu.VMEM(free.shape, jnp.int32), pltpu.VMEM(match.shape, jnp.int32),
            pltpu.VMEM(rhs.shape, F32), pltpu.SemaphoreType.DMA((5,)),
        ],
        compiler_params=params(PACK_MB),
        name="pack",
    )(rows, modes, free, match, rhs)


def frame_kernel(
    lines, slots, place_ref, own_ref, west_ref, north_ref, rhs_ref,
    mask_ref, t_high_ref, t_low_ref, g_high_ref, g_low_ref, gives_ref, takes_ref,
    coarse_ref, pieces_ref,
    table_ref, held_ref,
):
    cases = mask_ref.shape[1]
    span = MODES * lines[1]
    modes = [
        own_ref[16 * face + 8 : 16 * face + 8 + MODES, side * slots : (side + 1) * slots]
        for face in range(2)
        for side in range(2)
    ]
    no_north, no_west = place_ref[4] != 0, place_ref[5] != 0
    west = jnp.where(no_west, 0.0, west_ref[...])
    north = jnp.where(no_north, 0.0, north_ref[...])
    table_ref[...] = jnp.zeros_like(table_ref)
    masks = [
        own_ref[6:7, :slots], own_ref[22:23, :slots],
        west[6:7, :slots], north[6:7, :slots],
    ]
    entries = [
        (0, 0, modes[0]), (0, 1, modes[2]),
        (1, 0, modes[1]), (2, 1, modes[3]),
        (3, 2, west[8 : 8 + MODES, :slots]), (0, 2, west[8 : 8 + MODES, slots : 2 * slots]),
        (4, 3, north[8 : 8 + MODES, :slots]), (0, 3, north[8 : 8 + MODES, slots : 2 * slots]),
    ]
    for member, face, values in entries:
        table_ref[member * GROUP : member * GROUP + MODES, face * slots : (face + 1) * slots] = (
            values * masks[face]
        )
    table = table_ref[...]
    high, low = split(table[:TROWS])
    t_high_ref[...] = high
    t_low_ref[...] = low
    high, low = split(table.T)
    g_high_ref[...] = high
    g_low_ref[...] = low
    for face in range(4):
        spread = jnp.broadcast_to(masks[face], (cases, slots))
        mask_ref[face * slots : (face + 1) * slots, :] = spread.T
    order = lax.broadcasted_iota(jnp.int32, (slots, slots), 0).astype(F32)
    for side in range(2):
        moves = jnp.where(order == own_ref[16 * side + 7 : 16 * side + 8, :slots], 1.0, 0.0)
        gives_ref[side] = moves.astype(BF16)
        takes_ref[side] = moves.T.astype(BF16)
    coarse_ref[...] = jnp.zeros_like(coarse_ref)
    members = [own_ref[at : at + MODES, :] for at in (0, 32, 40)]
    members += [west[0:MODES, :], north[0:MODES, :]]
    for member, values in enumerate(members):
        coarse_ref[member * GROUP : member * GROUP + MODES, :] = values
    edge = jnp.zeros((ROWS, span), F32)
    padded = jnp.concatenate([edge, coarse_ref[...], edge], axis=1)
    for source in range(lines[1]):
        held_ref[source * MODES : (source + 1) * MODES, :] = rhs_ref[source, 0:MODES]
    tail = 3 * span - cases
    for line in range(lines[0]):
        first = line * span
        pieces_ref[line, 0:ROWS] = padded[:, first : first + cases]
        last = padded[:, first + cases : first + 3 * span]
        pieces_ref[line, ROWS : ROWS + GROUP] = jnp.zeros((GROUP, cases), F32)
        for member in range(MEMBERS):
            pieces_ref[line, ROWS : ROWS + GROUP, member * tail : (member + 1) * tail] = last[
                member * GROUP : (member + 1) * GROUP
            ]
        pieces_ref[line, ROWS + GROUP :] = held_ref[...]


def frame(lines, slots, place, own, west, north, rhs):
    size = 4 * slots
    width = own.shape[1]
    cases = rhs.shape[-1]
    span = MODES * lines[1]
    return pl.pallas_call(
        functools.partial(frame_kernel, lines, slots),
        in_specs=[SMEM_SPEC] + [VMEM_SPEC] * 4,
        out_specs=[VMEM_SPEC] * 9,
        out_shape=[
            jax.ShapeDtypeStruct((size, cases), F32),
            jax.ShapeDtypeStruct((TROWS, size), BF16),
            jax.ShapeDtypeStruct((TROWS, size), BF16),
            jax.ShapeDtypeStruct((size, 128), BF16),
            jax.ShapeDtypeStruct((size, 128), BF16),
            jax.ShapeDtypeStruct((2, slots, slots), BF16),
            jax.ShapeDtypeStruct((2, slots, slots), BF16),
            jax.ShapeDtypeStruct((ROWS, width), F32),
            jax.ShapeDtypeStruct((lines[0], ROWS + GROUP + span, cases), F32),
        ],
        scratch_shapes=[
            pltpu.VMEM((128, size), F32), pltpu.VMEM((span, cases), F32),
        ],
        compiler_params=params(12),
        name="frame",
    )(place, own, west, north, rhs)


def expansion(table_ref, columns):
    span = MODES * columns
    table_ref[...] = jnp.zeros_like(table_ref)
    row = lax.broadcasted_iota(jnp.int32, (MODES, MODES), 0)
    one = jnp.where(row == lax.broadcasted_iota(jnp.int32, (MODES, MODES), 1), 1.0, 0.0)
    for source in range(columns):
        places = [(0, source), (0, source + 1), (1, source), (0, source - 1), (-1, source)]
        for member, (down, column) in enumerate(places):
            if 0 <= column < columns:
                to = span * (1 + down) + MODES * column
                at = source * ROWS + member * GROUP
                table_ref[to : to + MODES, at : at + MODES] = one


def spread_kernel(
    received_ref, operator_ref, loads_in,
    high_ref, low_ref, a_high_ref, a_low_ref, loads_ref,
    tail_ref, held_ref, expand_ref, sems, loads_sem,
):
    size = operator_ref.shape[0]
    count = sems.shape[0]
    block = size // count
    copies = []
    for part in range(count):
        rows = pl.ds(part * block, block)
        copies.append(
            pltpu.make_async_copy(operator_ref.at[rows], held_ref.at[rows], sems.at[part])
        )
        copies[-1].start()
    loads_copy = pltpu.make_async_copy(loads_in, loads_ref, loads_sem)
    loads_copy.start()
    lines, _, cases = received_ref.shape
    tail = TAIL
    tail_ref[...] = jnp.zeros_like(tail_ref)
    packed = received_ref[:, ROWS : ROWS + GROUP, :]
    for member in range(MEMBERS):
        tail_ref[:, member * GROUP : (member + 1) * GROUP, 0:tail] = packed[
            :, :, member * tail : (member + 1) * tail
        ]
    expansion(expand_ref, expand_ref.shape[1] // ROWS)
    expand = expand_ref[...].astype(BF16)
    head = split(received_ref[:, 0:ROWS, :].reshape(lines * ROWS, cases))
    rest = split(tail_ref[...].reshape(lines * ROWS, cases))
    for first, last, out in zip(head, rest, (high_ref, low_ref)):
        result = mm(first, expand[0:cases]) + mm(last, expand[cases : 2 * cases])
        out[...] = result.astype(BF16)
    for part in range(count):
        copies[part].wait()
        rows = slice(part * block, (part + 1) * block)
        high, low = split(held_ref[rows, :])
        a_high_ref[rows, :] = high
        a_low_ref[rows, :] = low
    loads_copy.wait()


def spread(received, columns, operator, loads):
    lines, _, cases = received.shape
    shape = (lines * ROWS, columns * ROWS)
    size = operator.shape[0]
    return pl.pallas_call(
        spread_kernel,
        in_specs=[VMEM_SPEC] + [pl.BlockSpec(memory_space=pl.ANY)] * 2,
        out_specs=[VMEM_SPEC] * 5,
        out_shape=[jax.ShapeDtypeStruct(shape, BF16)] * 2
        + [jax.ShapeDtypeStruct((size, size), BF16)] * 2
        + [jax.ShapeDtypeStruct(loads.shape, F32)],
        scratch_shapes=[
            pltpu.VMEM((lines, ROWS, cases), F32), pltpu.VMEM((size, size), F32),
            pltpu.VMEM((2 * cases, columns * ROWS), F32),
            pltpu.SemaphoreType.DMA((8,)), pltpu.SemaphoreType.DMA,
        ],
        compiler_params=params(40),
        name="spread",
    )(received, operator, loads)


def solve_kernel(terms_ref, high_ref, low_ref, out_ref):
    terms = terms_ref[...]
    peers, rows, cases = terms.shape
    result = mm3(high_ref[...], low_ref[...], both(terms.reshape(peers * rows, cases)))
    kept = out_ref.shape[1]
    result = result.reshape(out_ref.shape[0], rows, cases)
    total = jnp.sum(terms, axis=0)
    place = lax.broadcasted_iota(jnp.int32, (rows, cases), 0)
    scalar = (place % GROUP) >= MODES
    if kept == PACKED:
        for member in range(MEMBERS):
            out_ref[:, member * MODES : (member + 1) * MODES, :] = result[
                :, member * GROUP : member * GROUP + MODES
            ]
        sums = total[MODES:GROUP]
        out_ref[:, MEMBERS * MODES : PACKED, :] = jnp.broadcast_to(
            sums[None], (out_ref.shape[0],) + sums.shape
        )
    else:
        out_ref[...] = jnp.where(scalar[None], total[None], result)[:, :kept]


def solve(terms, high, low, kept):
    lines = high.shape[0] // ROWS
    return pl.pallas_call(
        solve_kernel,
        in_specs=[VMEM_SPEC] * 3,
        out_specs=VMEM_SPEC,
        out_shape=jax.ShapeDtypeStruct((lines, kept, terms.shape[2]), F32),
        compiler_params=params(8),
        name="solve",
    )(terms, high, low)


def lift(alpha, g_high_ref, g_low_ref):
    filler = jnp.zeros((g_high_ref.shape[1] - alpha.shape[0], alpha.shape[1]), F32)
    pair = both(jnp.concatenate([alpha, filler], axis=0))
    return mm3(g_high_ref[...], g_low_ref[...], pair)


def field_image(r):
    even_x, even_y = r.parity[0] == 0, r.parity[1] == 0
    last_x, last_y = r.parity[2] != 0, r.parity[3] != 0
    slots = r.z_y.shape[1]

    def face(number, own, received):
        mask = r.mask[number * slots : (number + 1) * slots, :]
        return mask * (own + received)

    x_first, x_second = r.x_first[...], r.x_second[...]
    y_first, y_second = r.y_first[...], r.y_second[...]
    result = [
        face(0, r.z_y[0], jnp.where(even_y, y_first, jnp.where(last_y, 0.0, y_second))),
        face(1, r.z_x[0], jnp.where(even_x, x_first, jnp.where(last_x, 0.0, x_second))),
        face(2, r.z_y[1], jnp.where(even_y, y_second, y_first)),
        face(3, r.z_x[1], jnp.where(even_x, x_second, x_first)),
    ]
    return jnp.concatenate(result, axis=0)


def owned_image(r):
    last_x, last_y = r.parity[2] != 0, r.parity[3] != 0
    half = r.mask.shape[0] // 2
    east = r.z_y[0] + jnp.where(last_y, 0.0, r.y_first[...])
    south = r.z_x[0] + jnp.where(last_x, 0.0, r.x_first[...])
    return r.mask[:half, :] * jnp.concatenate([east, south], axis=0)


def member_alpha(total):
    place = lax.broadcasted_iota(jnp.int32, total.shape, 0)
    return jnp.where((place % GROUP) < MODES, total, 0.0)


def apply_faces(r, side, z_ref, first_ref, second_ref, loaded):
    slots = r.gives.shape[1]
    for index in (1, 0):
        face = side + 2 * index
        rows = slice(face * slots, (face + 1) * slots)
        out = mm3(r.a_high[rows, :], r.a_low[rows, :], r.pair[...])
        if index == 0 and loaded:
            out = out - r.loads[side]
        if index == 1:
            moved = mm(r.gives[side], both(out))
            columns = out.shape[1]
            out = -(moved[:, :columns] + moved[:, columns:])
        z_ref[index] = out
    if second_ref is None:
        first_ref[...] = z_ref[1]
    else:
        flip = r.parity[1 - side]
        first_ref[...] = z_ref[flip]
        second_ref[...] = z_ref[1 - flip]


def update_kernel(phase, names, *refs):
    r = SimpleNamespace(**dict(zip(names, refs)))
    slots = r.gives.shape[1]
    half = 2 * slots
    if phase == 0:
        lines, _, cases = r.received.shape
        span = r.rhs.shape[0] // lines
        for line in range(lines):
            r.rhs[line * span : (line + 1) * span, :] = r.received[line, ROWS + GROUP :]
        alpha = jnp.dot(
            r.coarse[...], r.rhs[...], precision=HIGHEST, preferred_element_type=F32
        )
        field = lift(alpha, r.g_high, r.g_low)
        r.lam_out[...] = field[:half]
    else:
        total = jnp.sum(r.parts[...], axis=0)
        if total.shape[0] == PACKED:
            for member in range(MEMBERS):
                at = member * GROUP
                r.grouped[at : at + MODES, :] = total[member * MODES : (member + 1) * MODES]
                r.grouped[at + MODES : at + GROUP, :] = total[MEMBERS * MODES : PACKED]
            total = r.grouped[...]
        moved = field_image(r) - lift(member_alpha(total), r.g_high, r.g_low)
        if phase == 1:
            field = moved
        elif phase == 2:
            norm = total[NORM_ROW : NORM_ROW + 1, :]
            energy = total[ENERGY_ROW : ENERGY_ROW + 1, :]
            step = norm / energy
            field = r.p[...] + step * moved
            r.q_out[...] = moved
            for place, value in enumerate((norm, energy, step)):
                r.scal_out[place : place + 1, :] = value
        else:
            step, beta, curvature, norm = step_terms(total, r.scal)
            image_p = moved + beta * r.q[...]
            field = r.p[...] + step * image_p
            r.q_out[...] = image_p
            for place, value in enumerate((norm, curvature, step, beta)):
                r.scal_out[place : place + 1, :] = value
        r.p_out[...] = field
    pair = both(field)
    r.pair[:half, :] = pair[:half]
    for side in range(2):
        rows = slice((2 + side) * slots, (3 + side) * slots)
        r.pair[rows, :] = (-mm(r.takes[side], pair[rows])).astype(BF16)
    second = None if phase == LAST else r.send_x_second
    apply_faces(r, 1, r.z_x_out, r.send_x_first, second, phase == 0)


def apply_kernel(phase, names, *refs):
    r = SimpleNamespace(**dict(zip(names, refs)))
    second = None if phase == LAST else r.send_y_second
    apply_faces(r, 0, r.z_y_out, r.send_y_first, second, phase == 0)


def terms_kernel(phase, names, *refs):
    r = SimpleNamespace(**dict(zip(names, refs)))
    slots = r.z_x.shape[1]
    half = 2 * slots
    terms = norm = energy = cross = 0.0
    if phase == 2:
        r.lam_out[...] = r.lam[...] + r.scal[2:3, :] * r.d[:half, :]
    if phase == 3:
        beta = r.scal[3:4, :]
        direction = r.p_old[...] + beta * r.d[...]
        r.d_out[...] = direction
        r.lam_out[...] = r.lam[...] + r.scal[2:3, :] * direction[:half]
    for face in range(4):
        rows = slice(face * slots, (face + 1) * slots)
        own, at = (r.z_x if face % 2 else r.z_y), face // 2
        out = own[at]
        terms = terms + mm3(r.t_high[:, rows], r.t_low[:, rows], both(out))
        if phase >= 1:
            mine = r.p[rows, :]
            energy = energy + jnp.sum(mine * out, axis=0, keepdims=True)
            if face < 2:
                norm = norm + jnp.sum(mine * mine, axis=0, keepdims=True)
        if phase >= 2:
            image = (r.z_x_old if face % 2 else r.z_y_old)[at]
            towards = r.d[rows, :]
            if phase == 3:
                image = image + beta * (r.z_x_older if face % 2 else r.z_y_older)[at]
                towards = r.d_out[rows, :]
            cross = cross + jnp.sum(mine * image + towards * out, axis=0, keepdims=True)
    terms = terms[0:ROWS, :]
    if phase >= 1:
        place = lax.broadcasted_iota(jnp.int32, terms.shape, 0)
        terms = jnp.where(place == NORM_ROW, norm, terms)
        terms = jnp.where(place == ENERGY_ROW, energy, terms)
        if phase >= 2:
            terms = jnp.where(place == CROSS_ROW, cross, terms)
    for peer in range(r.message.shape[0]):
        r.message[peer] = terms


def step_terms(total, scal_ref):
    norm = total[NORM_ROW : NORM_ROW + 1, :]
    energy = total[ENERGY_ROW : ENERGY_ROW + 1, :]
    cross = total[CROSS_ROW : CROSS_ROW + 1, :]
    beta = norm / scal_ref[0:1, :]
    curvature = energy + beta * cross + beta * beta * scal_ref[1:2, :]
    return norm / curvature, beta, curvature, norm


def call(kernel, name, inputs, shapes, scratch=None, halves=(), flops=0):
    scratch = scratch or {}
    keys = list(inputs) + list(shapes) + list(scratch)
    outs = pl.pallas_call(
        functools.partial(kernel, keys),
        in_specs=[VMEM_SPEC if v.shape != (FLAGS,) else SMEM_SPEC for v in inputs.values()],
        out_specs=[VMEM_SPEC] * len(shapes),
        out_shape=[
            jax.ShapeDtypeStruct(shape, BF16 if shape in halves else F32)
            for shape in shapes.values()
        ],
        scratch_shapes=list(scratch.values()),
        compiler_params=params(STEP_MB),
        cost_estimate=pl.CostEstimate(flops=flops, bytes_accessed=4096, transcendentals=0),
        name=name,
    )(*inputs.values())
    return SimpleNamespace(**dict(zip(shapes, outs)))


def step(phase, lines, table, before, exchange, state):
    slots = table.gives.shape[1]
    size = 4 * slots
    cases = table.mask.shape[1]
    face, pair, field = (slots, cases), (2, slots, cases), (size, cases)
    wide = (size, 2 * cases)
    half_flops = size * size * cases * 4
    inputs = dict(
        parity=table.parity, a_high=table.a_high, a_low=table.a_low, gives=table.gives,
        takes=table.takes, g_high=table.g_high, g_low=table.g_low,
    )
    inputs.update(state if before is None else dict(received_by(before), mask=table.mask))
    if phase == 2:
        inputs.update(p=state.p)
    if phase == 3:
        inputs.update(p=state.p, q=state.q, scal=state.scal)
    shapes = dict(pair=wide, z_x_out=pair, send_x_first=face)
    if phase < LAST:
        shapes.update(send_x_second=face)
    scratch = {}
    if phase == 0:
        shapes.update(lam_out=(2 * slots, cases))
        scratch = dict(rhs=pltpu.VMEM((MODES * lines[0] * lines[1], cases), F32))
    else:
        shapes.update(p_out=field)
        scratch = dict(grouped=pltpu.VMEM((ROWS, cases), F32))
    if phase >= 2:
        shapes.update(q_out=field, scal_out=(8, cases))
    update = call(
        functools.partial(update_kernel, phase), f"update{phase}", inputs, shapes, scratch,
        (wide,), half_flops,
    )
    inputs = dict(
        parity=table.parity, a_high=table.a_high, a_low=table.a_low, gives=table.gives,
        pair=update.pair,
    )
    if phase == 0:
        inputs.update(loads=state["loads"])
    shapes = dict(z_y_out=pair, send_y_first=face)
    if phase < LAST:
        shapes.update(send_y_second=face)
    apply = call(
        functools.partial(apply_kernel, phase), f"apply{phase}", inputs, shapes, flops=half_flops
    )
    inputs = dict(t_high=table.t_high, t_low=table.t_low, z_x=update.z_x_out, z_y=apply.z_y_out)
    shapes = dict(message=(lines[1], ROWS, cases))
    if phase:
        inputs.update(p=update.p_out)
    if phase >= 2:
        inputs.update(
            scal=update.scal_out, lam=state.lam, d=state.d, z_x_old=before.z_x, z_y_old=before.z_y
        )
        shapes.update(lam_out=(2 * slots, cases))
    if phase == 3:
        inputs.update(p_old=state.p, z_x_older=state.z_x_old, z_y_older=state.z_y_old)
        shapes.update(d_out=field)
    terms = call(
        functools.partial(terms_kernel, phase), f"terms{phase}", inputs, shapes,
        flops=half_flops // 4,
    )
    out = SimpleNamespace(**{**vars(update), **vars(apply), **vars(terms)})
    exchange(out, phase)
    return out


def received_by(out):
    inputs = dict(parts=out.parts, z_x=out.z_x, z_y=out.z_y, x_first=out.x_first, y_first=out.y_first)
    if out.x_second is not None:
        inputs.update(x_second=out.x_second, y_second=out.y_second)
    return inputs


def final_kernel(names, *refs):
    r = SimpleNamespace(**dict(zip(names, refs)))
    half = r.lam.shape[0]
    top = slice(0, half)
    total = jnp.sum(r.parts[...], axis=0)
    moved = owned_image(r) - lift(
        member_alpha(total), r.g_high.at[top], r.g_low.at[top]
    )
    step_size, beta, _, _ = step_terms(total, r.scal)
    direction = r.p[top, :] + beta * r.d[top, :]
    r.lam_out[...] = r.lam[...] + step_size * direction
    r.p_out[...] = r.p[top, :] + step_size * (moved + beta * r.q[top, :])


def shift(peers, by):
    return [(i, (i + by) % peers) for i in range(peers)]


def swap_first(peers):
    return [(i, i ^ 1) for i in range(peers)]


def swap_second(peers):
    return [(i, (i + (1 if i % 2 else -1)) % peers) for i in range(peers)]


def local(dual_ops, loads, coarse_rhs, coarse_modes, free_mask, face_match, coarse_rows):
    operator = dual_ops[0, 0]
    slots, cases = loads.shape[-2:]
    lines = (lax.axis_size("gx"), lax.axis_size("gy"))
    peers = lines[0] * lines[1]
    at = (lax.axis_index("gx"), lax.axis_index("gy"))
    parity = jnp.stack(
        [
            at[0] % 2, at[1] % 2, at[0] == lines[0] - 1, at[1] == lines[1] - 1,
            at[0] == 0, at[1] == 0,
        ]
    ).astype(jnp.int32)

    pack_east, pack_south, message, own = pack(
        coarse_rows[0, 0], coarse_modes[0, 0], free_mask[0, 0], face_match[0, 0],
        coarse_rhs[0, 0], lines[1],
    )
    west = lax.ppermute(pack_east, "gy", shift(lines[1], 1))
    north = lax.ppermute(pack_south, "gx", shift(lines[0], 1))
    message, parity = lax.optimization_barrier((message, parity))
    gathered = lax.all_to_all(message, "gy", 0, 0)
    gathered, west, north = lax.optimization_barrier((gathered, west, north))
    mask, t_high, t_low, g_high, g_low, gives, takes, coarse, pieces = frame(
        lines, slots, parity, own, west, north, gathered
    )
    received = lax.all_to_all(pieces, "gx", 0, 0)
    *solver, a_high, a_low, held_loads = spread(
        received, lines[1], operator, loads[0, 0]
    )
    table = SimpleNamespace(
        parity=parity, a_high=a_high, a_low=a_low, mask=mask, t_high=t_high, t_low=t_low,
        g_high=g_high, g_low=g_low, gives=gives, takes=takes,
    )

    def exchange(out, phase):
        last = phase == LAST
        kept = {0: PACKED, 1: PACKED, LAST: KEPT}.get(phase, ROWS)
        if last:
            halos = [
                lax.ppermute(out.send_x_first, "gx", shift(lines[0], -1)),
                lax.ppermute(out.send_y_first, "gy", shift(lines[1], -1)),
            ]
        else:
            halos = [
                lax.ppermute(out.send_x_first, "gx", swap_first(lines[0])),
                lax.ppermute(out.send_y_first, "gy", swap_first(lines[1])),
                lax.ppermute(out.send_x_second, "gx", swap_second(lines[0])),
                lax.ppermute(out.send_y_second, "gy", swap_second(lines[1])),
            ]
        terms = lax.all_to_all(out.message, "gy", 0, 0)
        terms, *halos = lax.optimization_barrier((terms, *halos))
        out.x_first, out.y_first = halos[:2]
        out.x_second, out.y_second = (None, None) if last else halos[2:]
        out.parts = lax.all_to_all(solve(terms, *solver, kept), "gx", 0, 0)
        out.z_x, out.z_y = out.z_x_out, out.z_y_out

    run = functools.partial(step, lines=lines, table=table, exchange=exchange)
    start = run(0, before=None, state=dict(received=received, coarse=coarse, loads=held_loads))
    first = run(1, before=start, state=None)
    second = run(
        2, before=first, state=SimpleNamespace(p=first.p_out, d=first.p_out, lam=start.lam_out)
    )
    third = run(
        3, before=second,
        state=SimpleNamespace(
            p=second.p_out, d=first.p_out, q=second.q_out, scal=second.scal_out,
            lam=second.lam_out, z_x_old=first.z_x, z_y_old=first.z_y,
        ),
    )
    half = (2 * slots, cases)
    out = call(
        final_kernel, "final",
        dict(
            received_by(third), parity=parity, mask=mask, g_high=g_high, g_low=g_low,
            p=third.p_out, d=third.d_out, q=third.q_out, scal=third.scal_out, lam=third.lam_out,
        ),
        dict(lam_out=half, p_out=half),
    )
    shape = (1, 1, 2, slots, cases)
    return out.lam_out.reshape(shape), out.p_out.reshape(shape)


def solution(mesh):
    in_specs = (
        P("gx", "gy", None, None),
        P("gx", "gy", None, None, None),
        P("gx", "gy", None, None),
        P("gx", "gy", None, None, None, None),
        P("gx", "gy", None, None),
        P("gx", "gy", None, None),
        P("gx", "gy", None, None, None),
    )
    out_specs = (P("gx", "gy", None, None, None), P("gx", "gy", None, None, None))
    return jax.shard_map(local, mesh=mesh, in_specs=in_specs, out_specs=out_specs, check_vma=False)
```
